128 devices in a mesh: node: 16 (over x, z), local: 8 (over y, core).
Axes of the slice: x: 4, y: 4, z: 4, core: 2. Of those that a mesh axis runs over, the one named last changes fastest.
Arguments:
- tokens: bfloat16 [32768, 7168], P(('node', 'local')), may hold values from -6 to 6
- out_grad: bfloat16 [32768, 7168], P(('node', 'local')), may hold values from -6 to 6
- route_ids: int32 [32768, 8], P(('node', 'local')), may hold values from 0 to 383, as said below
- route_gates: bfloat16 [32768, 8], P(('node', 'local')), may hold values from 0.049804688 to 0.5
- w_gate: bfloat16 [16, 7168, 1024], P('node', None, 'local'), may hold values from -0.0625 to 0.0625
- w_up: bfloat16 [16, 7168, 1024], P('node', None, 'local'), may hold values from -0.0625 to 0.0625
- w_down: bfloat16 [16, 1024, 7168], P('node', 'local'), may hold values from -0.1875 to 0.1875
Outputs:
- token_grad: bfloat16 [32768, 7168], P(('node', 'local'))
- gate_grad: float32 [32768, 8], P(('node', 'local'))
- grad_w_gate: bfloat16 [16, 7168, 1024], P('node', None, 'local')
- grad_w_up: bfloat16 [16, 7168, 1024], P('node', None, 'local')
- grad_w_down: bfloat16 [16, 1024, 7168], P('node', 'local')
The draws below stay inside these ranges and needn't reach their ends.
Inputs may be any that keep to these rules, and one draw needn't show every extreme that they name: `route_ids`: each row names 8 different experts, at most one of them below 16. Among the 256 rows of one device at most 4 name any one expert below 16; in every draw one expert below 16 is named by exactly 4 rows of every device.
All inputs are finite; a program needn't handle non-finite values.
Results may differ from the reference program's by a relative error of at most 0.0058.
Values may be sent and summed in bfloat16 or wider, within the bound.
A program may use at most 192 MiB of HBM per device.

```python
import jax
import jax.numpy as jnp
from jax import lax

D = 7168
FF = 1024
ALL_EXPERTS = 384
TOPK = 8
CAP = 4
TOK_DEV = 256
EXPERTS = 16
TOKENS = 32768
N_NODE = 16
N_LOCAL = 8


def draw_route_ids(key, part):
    key = jax.random.fold_in(key, 7)
    keys = jax.random.split(key, 6)
    devices = TOKENS // TOK_DEV
    group = ALL_EXPERTS // TOPK
    favored = jax.random.randint(keys[0], (), 0, EXPERTS)
    counts = jax.random.randint(keys[1], (devices, EXPERTS), 0, CAP + 1)
    counts = jnp.where(jnp.arange(EXPERTS)[None, :] == favored, CAP, counts)
    ends = jnp.cumsum(counts, axis=1)
    ranking = jax.random.randint(keys[2], (devices, TOK_DEV), 0, TOK_DEV) * TOK_DEV + jnp.arange(TOK_DEV)[None, :]
    placing = jnp.argsort(jnp.argsort(ranking, axis=1), axis=1)
    which = jnp.sum((placing[:, :, None] >= ends[:, None, :]).astype(jnp.int32), axis=2)
    spare = jax.random.randint(keys[3], (devices, TOK_DEV), EXPERTS, group)
    first = jnp.where(which < EXPERTS, which, spare)
    others = jnp.arange(1, TOPK)[None, None, :] * group + jax.random.randint(keys[4], (devices, TOK_DEV, TOPK - 1), 0, group)
    ordered = jnp.concatenate([first[:, :, None], others], axis=2)
    mixing = jax.random.randint(keys[5], (devices, TOK_DEV, TOPK), 0, 64) * TOPK + jnp.arange(TOPK)[None, None, :]
    shuffle = jnp.argsort(mixing, axis=2)
    chosen = jnp.take_along_axis(ordered, shuffle, axis=2)
    return chosen.reshape(TOKENS, TOPK).astype(jnp.int32)


def shard_levels(own_key, shape, cuts, low, top_value):
    loudness = 1.0
    for axis_at, parts in cuts:
        heights = jax.random.uniform(jax.random.fold_in(jax.random.fold_in(own_key, 6), axis_at), (parts,), jnp.float32, low / len(cuts), top_value / len(cuts))
        loudness = loudness * jnp.repeat(jnp.exp(heights), shape[axis_at] // parts).reshape((-1,) + (1,) * (len(shape) - 1 - axis_at))
    return loudness


def centred(stream_key, shape, width, limit, cuts=(), held_as=jnp.bfloat16):
    entries = width * jax.random.normal(stream_key, shape, jnp.float32)
    if cuts:
        entries = entries * shard_levels(stream_key, shape, cuts, -0.22, 0.18)
    return jnp.clip(entries, -limit, limit).astype(held_as)


def setup_inputs(seed: int = 0) -> dict:
    arg_keys = jax.random.split(jax.random.key(seed), 8)
    tokens = centred(arg_keys[0], (TOKENS, D), 1.0, 6.0, ((0, 128),))
    out_grad = centred(arg_keys[1], (TOKENS, D), 1.0, 6.0, ((0, 128),))
    route_ids = draw_route_ids(jax.random.fold_in(arg_keys[7], 71), 0)
    route_gates = jnp.clip(0.049804688 + 0.4501953 * jax.random.uniform(arg_keys[3], (TOKENS, TOPK), jnp.float32) ** shard_levels(arg_keys[3], (TOKENS, TOPK), ((0, 128),), -0.2, 0.2), 0.049804688, 0.5).astype(jnp.bfloat16)
    w_gate = centred(arg_keys[4], (EXPERTS, D, FF), D ** -0.5, 0.0625, ((0, 16), (2, 8)))
    w_up = centred(arg_keys[5], (EXPERTS, D, FF), D ** -0.5, 0.0625, ((0, 16), (2, 8)))
    w_down = centred(arg_keys[6], (EXPERTS, FF, D), FF ** -0.5, 0.1875, ((0, 16), (1, 8)))
    return dict(tokens=tokens, out_grad=out_grad, route_ids=route_ids, route_gates=route_gates, w_gate=w_gate, w_up=w_up, w_down=w_down)


def expert_pass(inputs, grads, gates, gate_mat, up_mat, down_mat):
    gate_pre = jnp.dot(inputs, gate_mat, preferred_element_type=jnp.float32)
    up_pre = jnp.dot(inputs, up_mat, preferred_element_type=jnp.float32)
    logistic = jax.nn.sigmoid(gate_pre)
    hidden = (gate_pre * logistic * up_pre).astype(jnp.bfloat16)
    expert_out = jnp.dot(hidden, down_mat, preferred_element_type=jnp.float32)
    scores = jnp.sum(expert_out * grads.astype(jnp.float32), axis=1)
    scaled_grad = (gates[:, None] * grads.astype(jnp.float32)).astype(jnp.bfloat16)
    hidden_grad = jnp.dot(scaled_grad, down_mat.T, preferred_element_type=jnp.float32)
    gate_delta = (hidden_grad * up_pre * logistic * (1.0 + gate_pre * (1.0 - logistic))).astype(jnp.bfloat16)
    up_delta = (hidden_grad * gate_pre * logistic).astype(jnp.bfloat16)
    grad_down = jnp.dot(hidden.T, scaled_grad, preferred_element_type=jnp.float32).astype(jnp.bfloat16)
    grad_gate = jnp.dot(inputs.T, gate_delta, preferred_element_type=jnp.float32).astype(jnp.bfloat16)
    grad_up = jnp.dot(inputs.T, up_delta, preferred_element_type=jnp.float32).astype(jnp.bfloat16)
    row_grads = jnp.dot(gate_delta, gate_mat.T, preferred_element_type=jnp.float32) + jnp.dot(up_delta, up_mat.T, preferred_element_type=jnp.float32)
    return scores, row_grads, grad_gate, grad_up, grad_down


def reference(tokens, out_grad, route_ids, route_gates, w_gate, w_up, w_down):
    is_held = route_ids < EXPERTS
    expert = jnp.sum(jnp.where(is_held, route_ids, 0), axis=1)
    inside = jnp.any(is_held, axis=1)
    tok_gate = jnp.sum(jnp.where(is_held, route_gates.astype(jnp.float32), jnp.float32(0.0)), axis=1)
    row_count = N_NODE * N_LOCAL * CAP

    def visit(carried, expert_id):
        grad_total, score_total = carried
        chosen = inside & (expert == expert_id)
        picked = jnp.nonzero(chosen, size=row_count, fill_value=0)[0].astype(jnp.int32)
        valid = jnp.arange(row_count) < jnp.sum(chosen.astype(jnp.int32))
        inputs = jnp.where(valid[:, None], tokens[picked], jnp.zeros((), jnp.bfloat16))
        grads = jnp.where(valid[:, None], out_grad[picked], jnp.zeros((), jnp.bfloat16))
        gates = jnp.where(valid, tok_gate[picked], jnp.float32(0.0))
        scores, row_grads, grad_gate, grad_up, grad_down = expert_pass(inputs, grads, gates, w_gate[expert_id], w_up[expert_id], w_down[expert_id])
        grad_total = grad_total.at[picked].add(jnp.where(valid[:, None], row_grads, jnp.float32(0.0)))
        score_total = score_total.at[picked].add(jnp.where(valid, scores, jnp.float32(0.0)))
        return (grad_total, score_total), (grad_gate, grad_up, grad_down)

    start = (jnp.zeros((TOKENS, D), jnp.float32), jnp.zeros((TOKENS,), jnp.float32))
    (grad_total, score_total), (grad_w_gate, grad_w_up, grad_w_down) = lax.scan(visit, start, jnp.arange(EXPERTS).astype(jnp.int32))
    token_grad = grad_total.astype(jnp.bfloat16)
    gate_grad = jnp.where(is_held, score_total[:, None], jnp.float32(0.0))
    return token_grad, gate_grad, grad_w_gate, grad_w_up, grad_w_down
```

```python
import functools

import jax
import jax.numpy as jnp
from jax import lax
from jax.experimental import pallas as pl
from jax.experimental.pallas import tpu as pltpu
from jax.sharding import PartitionSpec as P

MESH = pl.DeviceIdType.MESH
F32 = jnp.float32
BF16 = jnp.bfloat16

CAP = 4
TOK = 256
D = 7168
HALF = D // 2
QUART = D // 4
FFD = 128
NODES = 16
SIDE = 4
SCW = 128
RW = D + SCW
PH = 4
ROWS = 128


def iota(shape, dim):
    return lax.broadcasted_iota(jnp.int32, shape, dim)


def slot_targets(ids, gates):
    held = ids < NODES
    expert = jnp.sum(jnp.where(held, ids, 0).astype(F32), axis=1, keepdims=True)
    inside = jnp.sum(jnp.where(held, 1.0, 0.0), axis=1, keepdims=True) > 0.5
    gate = jnp.sum(jnp.where(held, gates.astype(F32), 0.0), axis=1, keepdims=True)
    lane = iota((TOK, 128), 1).astype(F32)
    one_hot = jnp.where((lane == expert) & inside, 1.0, 0.0)
    before = jnp.where(iota((TOK, TOK), 0) > iota((TOK, TOK), 1), 1.0, 0.0)
    ranks = jnp.dot(before.astype(BF16), one_hot.astype(BF16), preferred_element_type=F32)
    rank = jnp.sum(ranks * one_hot, axis=1, keepdims=True)
    target = jnp.where(inside, expert * CAP + rank, -1.0)
    return target, gate


def wanted(block, gx, gz):
    k = block >> 4
    p = k >> 2
    dx = p ^ (p >> 1)
    dz = k & 3
    node = ((gx - dx) & 3) * SIDE + ((gz - dz) & 3)
    return (node * CAP + (block & 3)).astype(F32), (block >> 2) & 3


def hi_lo(score):
    hi = score.astype(BF16).astype(F32)
    lane = iota(score.shape, 1)
    return jnp.where(lane < 64, hi, score - hi).astype(BF16)


def from_hi_lo(pair):
    wide = pair.astype(F32)
    return wide + pltpu.roll(wide, 64, 1)


def contract_cols(left, right):
    return lax.dot_general(left, right, (((1,), (1,)), ((), ())), preferred_element_type=F32)


def exchange_kernel(
    ids, gates, tok_hbm, og_hbm, wg_hbm, wu_hbm, wd_hbm,
    ret_hbm, gg_hbm, gu_hbm, gd_hbm,
    tok, og, pick, sraw, rraw, xg, wgu, wgup, wd,
    dl, dlt, hidt, score, psend, precv,
    rgf, o3s, o3r, j1s, j1r, j2s, j2r, fstk, rets, retr,
    ggo, guo, gdo, perm,
    ssem, rsem, lsem,
):
    node = lax.axis_index("node")
    loc = lax.axis_index("local")
    gx, gz = node // SIDE, node % SIDE
    y, c = loc // 2, loc % 2
    up = (node, ((y + 1) % 4) * 2 + c)
    down = (node, ((y + 3) % 4) * 2 + c)
    other = (node, y * 2 + 1 - c)

    def gray(k):
        p = k // 4
        return p ^ (p >> 1), k % 4

    def dest(k):
        dx, dz = gray(k)
        return (((gx + 4 - dx) % 4) * SIDE + (gz + 4 - dz) % 4, loc)

    def source(k):
        dx, dz = gray(k)
        return (((gx + dx) % 4) * SIDE + (gz + dz) % 4, loc)

    local = []

    def load(src, dst):
        copy = pltpu.make_async_copy(src, dst, lsem.at[len(local)])
        local.append(copy)
        copy.start()
        return copy

    ld_tok = load(tok_hbm, tok)
    ld_og = load(og_hbm, og)
    ld_wg = load(wg_hbm, wgu.at[:, pl.ds(0, FFD)])
    ld_wu = load(wu_hbm, wgu.at[:, pl.ds(FFD, FFD)])
    ld_wd = load(wd_hbm, wd)

    barrier = pltpu.get_barrier_semaphore()
    partners = [up, down, other] + [dest(k) for k in range(1, NODES)]
    for who in partners:
        pl.semaphore_signal(barrier, inc=1, device_id=who, device_id_type=MESH)

    remote = []

    def send(src, dst, who):
        i = len(remote)
        copy = pltpu.make_async_remote_copy(
            src_ref=src, dst_ref=dst, send_sem=ssem.at[i], recv_sem=rsem.at[i],
            device_id=who, device_id_type=MESH,
        )
        remote.append(copy)
        copy.start()
        return copy

    target, gate = slot_targets(ids[...], gates[...])
    eye = iota((TOK, TOK), 0) == iota((TOK, TOK), 1)
    target_row = jnp.sum(jnp.where(eye, target, 0.0), axis=0, keepdims=True)
    gate_row = jnp.sum(jnp.where(eye, gate, 0.0), axis=0, keepdims=True)
    want, quarter = wanted(iota((TOK, TOK), 0), gx, gz)
    hit = want == target_row
    for q in range(4):
        chosen = hit & (quarter == q)
        pick[q] = jnp.where(chosen, 1.0, 0.0).astype(BF16)
        pick[4 + q] = jnp.where(chosen, gate_row, 0.0).astype(BF16)
    pi, pj = iota((64, 64), 0), iota((64, 64), 1)
    swapped = ((pj >> 2) & 3) * 16 + (pj >> 4) * 4 + (pj & 3)
    perm[...] = jnp.where(pi == swapped, 1.0, 0.0).astype(BF16)

    def pick_rows(a, rows):
        @pl.loop(0, QUART // 256)
        def _(t):
            acc = jnp.zeros((TOK, 256), F32)
            for q in range(4):
                cols = pl.ds(pl.multiple_of(q * QUART + t * 256, 256), 256)
                acc += jnp.dot(pick[4 * a + q], rows[:, cols], preferred_element_type=F32)
            cols = pl.ds(pl.multiple_of(t * 256, 256), 256)
            sraw[a, :, cols] = acc.astype(BF16)
            rraw[a, 0:16, cols] = acc[0:16].astype(BF16)

    scatter = {}

    def send_raw(a):
        for k in range(1, NODES):
            part = (a, pl.ds(16 * k, 16))
            scatter[a, k] = send(sraw.at[part], rraw.at[part], dest(k))

    ld_tok.wait()
    pick_rows(0, tok)
    pl.semaphore_wait(barrier, len(partners))
    send_raw(0)
    ld_og.wait()
    pick_rows(1, og)
    send_raw(1)

    left, right = pl.ds(0, HALF), pl.ds(HALF, HALF)
    gath = {}

    def unit(u):
        return u % 2, (u // 2) * ROWS

    def spread(u):
        a, at = unit(u)
        p = u // 2
        for k in range(4 * p, 4 * p + 4):
            if k:
                scatter[a, k].wait_recv()
        rows = jnp.dot(perm[...], rraw[a, 64 * p:64 * p + 64, :], preferred_element_type=F32).astype(BF16)
        for q in range(4):
            xg[a, at:at + 16, q * QUART:(q + 1) * QUART] = rows[16 * q:16 * q + 16]
        mine = xg.at[a, pl.ds(at, 16)]
        gath[u, "u"] = send(mine, xg.at[a, pl.ds(at + 16, 16)], up)
        gath[u, "d"] = send(mine, xg.at[a, pl.ds(at + 32, 16)], down)
        gath[u, "c0"] = send(mine, xg.at[a, pl.ds(at + 64, 16)], other)

    def forward(u):
        a, at = unit(u)
        opp = pl.ds(at + 48, 16)
        gath[u, "u"].wait_recv()
        gath[u, "fu"] = send(xg.at[a, pl.ds(at + 16, 16), left], xg.at[a, opp, left], up)
        gath[u, "d"].wait_recv()
        gath[u, "fd"] = send(xg.at[a, pl.ds(at + 32, 16), right], xg.at[a, opp, right], down)
        gath[u, "c12"] = send(xg.at[a, pl.ds(at + 16, 32)], xg.at[a, pl.ds(at + 80, 32)], other)

    def opposite(u):
        a, at = unit(u)
        gath[u, "fu"].wait_recv()
        gath[u, "fd"].wait_recv()
        gath[u, "c3"] = send(xg.at[a, pl.ds(at + 48, 16)], xg.at[a, pl.ds(at + 112, 16)], other)

    back = {}

    def compute(p):
        for u in (2 * p, 2 * p + 1):
            for part in ("c0", "c12", "c3"):
                gath[u, part].wait_recv()
        at = p * ROWS
        pre = jnp.dot(xg[0, at:at + ROWS, :], wgu[...], preferred_element_type=F32)
        hidden_grad = contract_cols(xg[1, at:at + ROWS, :], wd[...])
        gate_pre, up_pre = pre[:, :FFD], pre[:, FFD:]
        logistic = jax.nn.sigmoid(gate_pre)
        silu = gate_pre * logistic
        hidden = (silu * up_pre).astype(BF16).astype(F32)
        gate_delta = hidden_grad * up_pre * logistic * (1.0 + gate_pre * (1.0 - logistic))
        up_delta = hidden_grad * silu
        part = jnp.sum(hidden * hidden_grad, axis=1, keepdims=True)
        part = jnp.broadcast_to(part, (ROWS, SCW))
        score[p] = part[0:64]
        dl[p, :, 0:FFD] = gate_delta[0:64].astype(BF16)
        dl[p, :, FFD:2 * FFD] = up_delta[0:64].astype(BF16)
        psend[p, :, 0:FFD] = gate_delta[64:128].astype(BF16)
        psend[p, :, FFD:2 * FFD] = up_delta[64:128].astype(BF16)
        psend[p, :, 2 * FFD:] = hi_lo(part[64:128])
        back[p, "c"] = send(psend.at[p], precv.at[p], other)
        dlt[0:FFD, at:at + ROWS] = gate_delta.T.astype(BF16)
        dlt[FFD:2 * FFD, at:at + ROWS] = up_delta.T.astype(BF16)
        hidt[:, at:at + ROWS] = hidden.T.astype(BF16)

    def row_grads(p):
        back[p, "c"].wait_recv()
        mine, theirs = dl[p], precv[p, :, 0:2 * FFD]
        total = score[p] + from_hi_lo(precv[p, :, 2 * FFD:])
        rgf[p, :, D:] = total[0:48]
        o3s[p, :, D:] = hi_lo(total[48:64])
        j2s[p, :, D:] = hi_lo(total[32:48])

        def tiles(lo, hi, ready):
            @pl.loop(lo, hi)
            def _(t):
                cols = pl.ds(pl.multiple_of(t * 512, 512), 512)
                grad = contract_cols(mine, wgu[cols, :]) + contract_cols(theirs, wgup[cols, :])
                rgf[p, :, cols] = grad[0:48]
                o3s[p, :, cols] = grad[48:64].astype(BF16)
                ready[p, :, cols] = grad[16:32].astype(BF16) if ready is j1s else grad[32:48].astype(BF16)

        tiles(0, 7, j1s)
        back[p, "ol"] = send(o3s.at[p, :, left], o3r.at[p, :, left], up)
        back[p, "j1l"] = send(j1s.at[p, :, left], j1r.at[p, :, left], down)
        tiles(7, 14, j2s)
        tail = pl.ds(HALF, RW - HALF)
        back[p, "or"] = send(o3s.at[p, :, tail], o3r.at[p, :, tail], down)
        back[p, "j2r"] = send(j2s.at[p, :, tail], j2r.at[p, :, tail], up)

    def merge(p):
        back[p, "ol"].wait_recv()
        j2s[p, :, 0:HALF] = (rgf[p, 32:48, 0:HALF] + o3r[p, :, 0:HALF].astype(F32)).astype(BF16)
        back[p, "j2l"] = send(j2s.at[p, :, left], j2r.at[p, :, left], up)
        back[p, "or"].wait_recv()
        j1s[p, :, HALF:D] = (rgf[p, 16:32, HALF:D] + o3r[p, :, HALF:D].astype(F32)).astype(BF16)
        j1s[p, :, D:] = hi_lo(rgf[p, 16:32, D:] + from_hi_lo(o3r[p, :, D:]))
        tail = pl.ds(HALF, RW - HALF)
        back[p, "j1r"] = send(j1s.at[p, :, tail], j1r.at[p, :, tail], down)

    def home(p):
        for part in ("j1l", "j1r", "j2l", "j2r"):
            back[p, part].wait_recv()
        for q in range(4):
            cols = slice(q * QUART, (q + 1) * QUART)
            full = rgf[p, 0:16, cols] + j1r[p, :, cols].astype(F32) + j2r[p, :, cols].astype(F32)
            fstk[16 * q:16 * q + 16, 0:QUART] = full.astype(BF16)
        total = hi_lo(rgf[p, 0:16, D:] + from_hi_lo(j1r[p, :, D:]) + from_hi_lo(j2r[p, :, D:]))
        for q in range(4):
            fstk[16 * q:16 * q + 16, QUART:] = total
        block = jnp.dot(perm[...], fstk[...], preferred_element_type=F32).astype(BF16)
        rets[64 * p:64 * p + 64, :] = block
        if p == 0:
            retr[0:16, :] = block[0:16]
        for k in range(4 * p, 4 * p + 4):
            if k:
                part = pl.ds(16 * k, 16)
                back[k] = send(rets.at[part], retr.at[part], source(k))

    outs = []

    def store(src, dst):
        copy = pltpu.make_async_copy(src, dst, lsem.at[len(local)])
        local.append(copy)
        outs.append(copy)
        copy.start()

    def weight_grads(lo, hi):
        @pl.loop(lo, hi)
        def _(t):
            cols = pl.ds(pl.multiple_of(t * 512, 512), 512)
            both = jnp.dot(dlt[...], xg[0, :, cols], preferred_element_type=F32)
            ggo[cols, :] = both[0:FFD].T.astype(BF16)
            guo[cols, :] = both[FFD:].T.astype(BF16)
            gdo[:, cols] = jnp.dot(hidt[...], xg[1, :, cols], preferred_element_type=F32).astype(BF16)

    spread(0)
    spread(1)
    ld_wg.wait()
    ld_wu.wait()
    weights = send(wgu, wgup, other)
    forward(0)
    spread(2)
    forward(1)
    opposite(0)
    spread(3)
    ld_wd.wait()
    forward(2)
    opposite(1)
    spread(4)
    compute(0)
    forward(3)
    opposite(2)
    spread(5)
    weights.wait_recv()
    row_grads(0)
    forward(4)
    opposite(3)
    spread(6)
    compute(1)
    merge(0)
    forward(5)
    opposite(4)
    spread(7)
    row_grads(1)
    home(0)
    forward(6)
    opposite(5)
    compute(2)
    merge(1)
    forward(7)
    opposite(6)
    row_grads(2)
    home(1)
    opposite(7)
    compute(3)
    merge(2)
    row_grads(3)
    home(2)
    weight_grads(0, 4)
    merge(3)
    weight_grads(4, 8)
    home(3)
    weight_grads(8, 14)
    store(ggo, gg_hbm)
    store(guo, gu_hbm)
    store(gdo, gd_hbm)
    for k in range(1, NODES):
        back[k].wait_recv()
    store(retr, ret_hbm)
    for copy in remote:
        copy.wait_send()
    for copy in outs:
        copy.wait()


def scatter_kernel(ids, gates, ret, grad, gate_grad):
    node = lax.axis_index("node")
    gx, gz = node // SIDE, node % SIDE
    target, gate = slot_targets(ids[...], gates[...])
    want, quarter = wanted(iota((TOK, TOK), 1), gx, gz)
    hit = want == target
    q = pl.program_id(0)
    chosen = jnp.where(hit & (quarter == q), 1.0, 0.0).astype(BF16)
    grad[...] = jnp.dot(chosen, ret[:, 0:QUART], preferred_element_type=F32).astype(BF16)

    @pl.when(q == 0)
    def _():
        pair = jnp.dot(chosen, ret[:, QUART:], preferred_element_type=F32)
        lane = iota(pair.shape, 1)
        total = jnp.sum(jnp.where((lane & 63) == 0, pair, 0.0), axis=1, keepdims=True)
        scaled = total / jnp.where(gate > 0.0, gate, 1.0)
        gate_grad[...] = jnp.where(ids[...] < NODES, scaled, 0.0)


def body(tokens, out_grad, route_ids, route_gates, w_gate, w_up, w_down):
    any_space = pl.BlockSpec(memory_space=pl.ANY)
    in_vmem = pl.BlockSpec(memory_space=pltpu.VMEM)
    copies = 30 + 8 * 7 + 4 + 4 * 6 + 15 + 1
    ret, gg, gu, gd = pl.pallas_call(
        exchange_kernel,
        out_shape=(
            jax.ShapeDtypeStruct((TOK, QUART + SCW), BF16),
            jax.ShapeDtypeStruct((D, FFD), BF16),
            jax.ShapeDtypeStruct((D, FFD), BF16),
            jax.ShapeDtypeStruct((FFD, D), BF16),
        ),
        in_specs=[in_vmem, in_vmem] + [any_space] * 5,
        out_specs=(any_space,) * 4,
        scratch_shapes=[
            pltpu.VMEM((TOK, D), BF16),
            pltpu.VMEM((TOK, D), BF16),
            pltpu.VMEM((8, TOK, TOK), BF16),
            pltpu.VMEM((2, TOK, QUART), BF16),
            pltpu.VMEM((2, TOK, QUART), BF16),
            pltpu.VMEM((2, PH * ROWS, D), BF16),
            pltpu.VMEM((D, 2 * FFD), BF16),
            pltpu.VMEM((D, 2 * FFD), BF16),
            pltpu.VMEM((FFD, D), BF16),
            pltpu.VMEM((PH, 64, 2 * FFD), BF16),
            pltpu.VMEM((2 * FFD, PH * ROWS), BF16),
            pltpu.VMEM((FFD, PH * ROWS), BF16),
            pltpu.VMEM((PH, 64, SCW), F32),
            pltpu.VMEM((PH, 64, 2 * FFD + SCW), BF16),
            pltpu.VMEM((PH, 64, 2 * FFD + SCW), BF16),
            pltpu.VMEM((PH, 48, RW), F32),
            pltpu.VMEM((PH, 16, RW), BF16),
            pltpu.VMEM((PH, 16, RW), BF16),
            pltpu.VMEM((PH, 16, RW), BF16),
            pltpu.VMEM((PH, 16, RW), BF16),
            pltpu.VMEM((PH, 16, RW), BF16),
            pltpu.VMEM((PH, 16, RW), BF16),
            pltpu.VMEM((64, QUART + SCW), BF16),
            pltpu.VMEM((TOK, QUART + SCW), BF16),
            pltpu.VMEM((TOK, QUART + SCW), BF16),
            pltpu.VMEM((D, FFD), BF16),
            pltpu.VMEM((D, FFD), BF16),
            pltpu.VMEM((FFD, D), BF16),
            pltpu.VMEM((64, 64), BF16),
            pltpu.SemaphoreType.DMA((copies,)),
            pltpu.SemaphoreType.DMA((copies,)),
            pltpu.SemaphoreType.DMA((9,)),
        ],
        compiler_params=pltpu.CompilerParams(
            collective_id=0, has_side_effects=True, vmem_limit_bytes=60 * 2**20
        ),
        cost_estimate=pl.CostEstimate(
            flops=8 * 10**9, bytes_accessed=20 * 10**6, transcendentals=65536
        ),
        name="exchange",
    )(route_ids, route_gates, tokens, out_grad, w_gate[0], w_up[0], w_down[0])
    token_grad, gate_grad = pl.pallas_call(
        scatter_kernel,
        grid=(4,),
        out_shape=(
            jax.ShapeDtypeStruct((TOK, D), BF16),
            jax.ShapeDtypeStruct((TOK, 8), F32),
        ),
        in_specs=[
            pl.BlockSpec((TOK, 8), lambda q: (0, 0)),
            pl.BlockSpec((TOK, 8), lambda q: (0, 0)),
            pl.BlockSpec((TOK, QUART + SCW), lambda q: (0, 0)),
        ],
        out_specs=(
            pl.BlockSpec((TOK, QUART), lambda q: (0, q)),
            pl.BlockSpec((TOK, 8), lambda q: (0, 0)),
        ),
        compiler_params=pltpu.CompilerParams(vmem_limit_bytes=16 * 2**20),
        name="scatter",
    )(route_ids, route_gates, ret)
    return token_grad, gate_grad, gg[None], gu[None], gd[None]


def solution(mesh):
    return jax.shard_map(
        body,
        mesh=mesh,
        in_specs=(
            P(("node", "local"), None),
            P(("node", "local"), None),
            P(("node", "local"), None),
            P(("node", "local"), None),
            P("node", None, "local"),
            P("node", None, "local"),
            P("node", "local", None),
        ),
        out_specs=(
            P(("node", "local"), None),
            P(("node", "local"), None),
            P("node", None, "local"),
            P("node", None, "local"),
            P("node", "local", None),
        ),
        check_vma=False,
    )
```

```python
import functools

import jax
import jax.numpy as jnp
from jax import lax
from jax.experimental import pallas as pl
from jax.experimental.pallas import tpu as pltpu
from jax.sharding import PartitionSpec as P

MESH = pl.DeviceIdType.MESH
F32 = jnp.float32
BF16 = jnp.bfloat16

CAP = 4
TOK = 256
D = 7168
HALF = D // 2
QUART = D // 4
FFD = 128
NODES = 16
SIDE = 4
SCW = 128
RW = D + SCW
PH = 4
OFFSETS = (
    (0, 0), (1, 1), (3, 3), (1, 3), (3, 1), (0, 2), (2, 0), (2, 2),
    (1, 2), (3, 2), (2, 1), (2, 3), (0, 1), (0, 3), (1, 0), (3, 0),
)


def two_bits(values):
    word = sum(v << (2 * i) for i, v in enumerate(values))
    return word - 2**32 if word >= 2**31 else word


DX_BITS = two_bits([dx for dx, _ in OFFSETS])
DZ_BITS = two_bits([dz for _, dz in OFFSETS])
ROWS = 128


def iota(shape, dim):
    return lax.broadcasted_iota(jnp.int32, shape, dim)


def slot_targets(ids, gates):
    held = ids < NODES
    expert = jnp.sum(jnp.where(held, ids, 0).astype(F32), axis=0, keepdims=True)
    inside = jnp.sum(jnp.where(held, 1.0, 0.0), axis=0, keepdims=True) > 0.5
    gate = jnp.sum(jnp.where(held, gates.astype(F32), 0.0), axis=0, keepdims=True)
    row = iota((NODES, TOK), 0).astype(F32)
    one_hot = jnp.where((row == expert) & inside, 1.0, 0.0)
    before = jnp.where(iota((TOK, TOK), 0) < iota((TOK, TOK), 1), 1.0, 0.0)
    ranks = jnp.dot(one_hot.astype(BF16), before.astype(BF16), preferred_element_type=F32)
    rank = jnp.sum(ranks * one_hot, axis=0, keepdims=True)
    target = jnp.where(inside, expert * CAP + rank, -1.0)
    return target, gate


def wanted(block, gx, gz):
    k = block >> 4
    dx = lax.shift_right_logical(jnp.full(k.shape, DX_BITS, jnp.int32), 2 * k) & 3
    dz = lax.shift_right_logical(jnp.full(k.shape, DZ_BITS, jnp.int32), 2 * k) & 3
    node = ((gx - dx) & 3) * SIDE + ((gz - dz) & 3)
    return (node * CAP + (block & 3)).astype(F32), (block >> 2) & 3


def hi_lo(score):
    hi = score.astype(BF16).astype(F32)
    lane = iota(score.shape, 1)
    return jnp.where(lane < 64, hi, score - hi).astype(BF16)


def from_hi_lo(pair):
    wide = pair.astype(F32)
    return wide + pltpu.roll(wide, 64, 1)


def contract_cols(left, right):
    return lax.dot_general(left, right, (((1,), (1,)), ((), ())), preferred_element_type=F32)


def exchange_kernel(
    ids_hbm, gates_hbm, tok_hbm, og_hbm, wg_hbm, wu_hbm, wd_hbm,
    retr, ggo, guo, gdo,
    ids, gates, tok, og, pick, sraw, rraw, rx, xg, wgu, wgup, wd,
    dl, dlt, hidt, score, psend, precv,
    rgf, o3s, o3r, j1s, j1r, j2s, j2r, fstk, rets, perm, pre_ref,
    ssem, rsem, lsem,
):
    node = lax.axis_index("node")
    loc = lax.axis_index("local")
    gx, gz = node // SIDE, node % SIDE
    y, c = loc // 2, loc % 2
    up = (node, ((y + 1) % 4) * 2 + c)
    down = (node, ((y + 3) % 4) * 2 + c)
    other = (node, y * 2 + 1 - c)

    def dest(k):
        dx, dz = OFFSETS[k]
        return (((gx + 4 - dx) % 4) * SIDE + (gz + 4 - dz) % 4, loc)

    def source(k):
        dx, dz = OFFSETS[k]
        return (((gx + dx) % 4) * SIDE + (gz + dz) % 4, loc)

    barrier = pltpu.get_barrier_semaphore()
    partners = [up, down, other] + [dest(k) for k in range(1, NODES)]
    for who in partners:
        pl.semaphore_signal(barrier, inc=1, device_id=who, device_id_type=MESH)

    local = []

    def load(src, dst):
        copy = pltpu.make_async_copy(src, dst, lsem.at[len(local)])
        local.append(copy)
        copy.start()
        return copy

    ld_ids = load(ids_hbm, ids)
    ld_gates = load(gates_hbm, gates)
    ld_tok = load(tok_hbm, tok)
    ld_og = load(og_hbm, og)

    remote = []

    def send(src, dst, who):
        i = len(remote)
        copy = pltpu.make_async_remote_copy(
            src_ref=src, dst_ref=dst, send_sem=ssem.at[i], recv_sem=rsem.at[i],
            device_id=who, device_id_type=MESH,
        )
        remote.append(copy)
        copy.start()
        return copy

    ld_ids.wait()
    ld_gates.wait()
    target, gate = slot_targets(ids[...], gates[...])
    want, quarter = wanted(iota((TOK, TOK), 0), gx, gz)
    hit = want == target
    for q in range(4):
        chosen = hit & (quarter == q)
        pick[q] = jnp.where(chosen, 1.0, 0.0).astype(BF16)
        pick[4 + q] = jnp.where(chosen, gate, 0.0).astype(BF16)
    pi, pj = iota((64, 64), 0), iota((64, 64), 1)
    swapped = ((pj >> 2) & 3) * 16 + (pj >> 4) * 4 + (pj & 3)
    perm[...] = jnp.where(pi == swapped, 1.0, 0.0).astype(BF16)

    def pick_rows(a, rows, lo, hi):
        @pl.loop(0, QUART // 256)
        def _(t):
            acc = jnp.zeros((hi - lo, 256), F32)
            for q in range(4):
                cols = pl.ds(pl.multiple_of(q * QUART + t * 256, 256), 256)
                acc += jnp.dot(pick[4 * a + q, lo:hi, :], rows[:, cols], preferred_element_type=F32)
            cols = pl.ds(pl.multiple_of(t * 256, 256), 256)
            sraw[a, lo:hi, cols] = acc.astype(BF16)
            if lo == 0:
                rx[a, 0, 0:16, cols] = acc[0:16].astype(BF16)

    scatter = {}

    def send_part(u):
        a, p = u % 2, u // 2
        for k in range(4 * p, 4 * p + 4):
            if k:
                part = pl.ds(16 * k, 16)
                land = rraw.at[a, part] if p else rx.at[a, 0, part]
                scatter[a, k] = send(sraw.at[a, part], land, dest(k))

    gath = {}

    def own_block(a, name, rows):
        block = rx.at[a, 0, rows]
        gath[a, "u" + name] = send(block, rx.at[a, 1, rows], up)
        gath[a, "d" + name] = send(block, rx.at[a, 2, rows], down)
        gath[a, "c0" + name] = send(block, rx.at[a, 4, rows], other)

    def rest(a):
        for k in range(1, 4):
            scatter[a, k].wait_recv()
        own_block(a, "", pl.ds(16, 48))

    ld_tok.wait()
    pick_rows(0, tok, 0, 64)
    pl.semaphore_wait(barrier, len(partners))
    own_block(0, "first", pl.ds(0, 16))
    send_part(0)
    ld_og.wait()
    ld_wg = load(wg_hbm, wgu.at[:, pl.ds(0, FFD)])
    ld_wu = load(wu_hbm, wgu.at[:, pl.ds(FFD, FFD)])
    ld_wd = load(wd_hbm, wd)
    pick_rows(1, og, 0, 64)
    own_block(1, "first", pl.ds(0, 16))
    send_part(1)
    pick_rows(0, tok, 64, TOK)

    left, right = pl.ds(0, HALF), pl.ds(HALF, HALF)

    def unit(u):
        return u % 2, (u // 2) * ROWS

    def spread(u):
        a, at = unit(u)
        p = u // 2
        for k in range(4 * p, 4 * p + 4):
            if k:
                scatter[a, k].wait_recv()
        rows = jnp.dot(perm[...], rraw[a, 64 * p:64 * p + 64, :], preferred_element_type=F32).astype(BF16)
        for q in range(4):
            xg[a, at:at + 16, q * QUART:(q + 1) * QUART] = rows[16 * q:16 * q + 16]
        mine = xg.at[a, pl.ds(at, 16)]
        gath[u, "u"] = send(mine, xg.at[a, pl.ds(at + 16, 16)], up)
        gath[u, "d"] = send(mine, xg.at[a, pl.ds(at + 32, 16)], down)
        gath[u, "c0"] = send(mine, xg.at[a, pl.ds(at + 64, 16)], other)

    def forward(u):
        a, at = unit(u)
        if u < 2:
            near, far = pl.ds(0, QUART // 2), pl.ds(QUART // 2, QUART // 2)
            gath[u, "ufirst"].wait_recv()
            gath[u, "u"].wait_recv()
            gath[u, "fu"] = send(rx.at[a, 1, :, near], rx.at[a, 3, :, near], up)
            gath[u, "dfirst"].wait_recv()
            gath[u, "d"].wait_recv()
            gath[u, "fd"] = send(rx.at[a, 2, :, far], rx.at[a, 3, :, far], down)
            gath[u, "c12"] = send(rx.at[a, pl.ds(1, 2)], rx.at[a, pl.ds(5, 2)], other)
            return
        opp = pl.ds(at + 48, 16)
        gath[u, "u"].wait_recv()
        gath[u, "fu"] = send(xg.at[a, pl.ds(at + 16, 16), left], xg.at[a, opp, left], up)
        gath[u, "d"].wait_recv()
        gath[u, "fd"] = send(xg.at[a, pl.ds(at + 32, 16), right], xg.at[a, opp, right], down)
        gath[u, "c12"] = send(xg.at[a, pl.ds(at + 16, 32)], xg.at[a, pl.ds(at + 80, 32)], other)

    def opposite(u):
        a, at = unit(u)
        gath[u, "fu"].wait_recv()
        gath[u, "fd"].wait_recv()
        if u < 2:
            gath[u, "c3"] = send(rx.at[a, 3], rx.at[a, 7], other)
            return
        gath[u, "c3"] = send(xg.at[a, pl.ds(at + 48, 16)], xg.at[a, pl.ds(at + 112, 16)], other)

    back = {}

    def arrived(u):
        a, at = unit(u)
        for part in ("c0", "c12", "c3"):
            gath[u, part].wait_recv()
        if u < 2:
            gath[u, "c0first"].wait_recv()

            @pl.loop(0, 8)
            def _(b):
                rows = jnp.dot(perm[...], rx[a, b], preferred_element_type=F32).astype(BF16)
                to = pl.ds(pl.multiple_of(b * 16, 16), 16)
                for q in range(4):
                    xg[a, to, q * QUART:(q + 1) * QUART] = rows[16 * q:16 * q + 16]

    def project(p):
        arrived(2 * p)
        at = p * ROWS
        pre_ref[...] = jnp.dot(xg[0, at:at + ROWS, :], wgu[...], preferred_element_type=F32)

    def compute(p):
        arrived(2 * p + 1)
        at = p * ROWS
        pre = pre_ref[...]
        hidden_grad = contract_cols(xg[1, at:at + ROWS, :], wd[...])
        gate_pre, up_pre = pre[:, :FFD], pre[:, FFD:]
        logistic = jax.nn.sigmoid(gate_pre)
        silu = gate_pre * logistic
        hidden = (silu * up_pre).astype(BF16).astype(F32)
        gate_delta = hidden_grad * up_pre * logistic * (1.0 + gate_pre * (1.0 - logistic))
        up_delta = hidden_grad * silu
        part = jnp.sum(hidden * hidden_grad, axis=1, keepdims=True)
        part = jnp.broadcast_to(part, (ROWS, SCW))
        score[p] = part[0:64]
        dl[p, :, 0:FFD] = gate_delta[0:64].astype(BF16)
        dl[p, :, FFD:2 * FFD] = up_delta[0:64].astype(BF16)
        psend[p, :, 0:FFD] = gate_delta[64:128].astype(BF16)
        psend[p, :, FFD:2 * FFD] = up_delta[64:128].astype(BF16)
        psend[p, :, 2 * FFD:] = hi_lo(part[64:128])
        back[p, "c"] = send(psend.at[p], precv.at[p], other)
        dlt[0:FFD, at:at + ROWS] = gate_delta.T.astype(BF16)
        dlt[FFD:2 * FFD, at:at + ROWS] = up_delta.T.astype(BF16)
        hidt[:, at:at + ROWS] = hidden.T.astype(BF16)

    tail = pl.ds(HALF, RW - HALF)

    def row_tiles(p, lo, hi, ready):
        mine, theirs = dl[p], precv[p, :, 0:2 * FFD]

        @pl.loop(lo, hi)
        def _(t):
            cols = pl.ds(pl.multiple_of(t * 512, 512), 512)
            grad = contract_cols(mine, wgu[cols, :]) + contract_cols(theirs, wgup[cols, :])
            rgf[p % 2, :, cols] = grad[0:48]
            o3s[p, :, cols] = grad[48:64].astype(BF16)
            ready[p, :, cols] = grad[16:32].astype(BF16) if ready is j1s else grad[32:48].astype(BF16)

    def row_left(p):
        back[p, "c"].wait_recv()
        total = score[p] + from_hi_lo(precv[p, :, 2 * FFD:])
        rgf[p % 2, :, D:] = total[0:48]
        o3s[p, :, D:] = hi_lo(total[48:64])
        j2s[p, :, D:] = hi_lo(total[32:48])
        row_tiles(p, 0, 7, j1s)

    def row_right(p):
        row_tiles(p, 7, 14, j2s)

    def send_left(p):
        back[p, "ol"] = send(o3s.at[p, :, left], o3r.at[p, :, left], up)
        back[p, "j1l"] = send(j1s.at[p, :, left], j1r.at[p, :, left], down)

    def send_right(p):
        back[p, "or"] = send(o3s.at[p, :, tail], o3r.at[p, :, tail], down)
        back[p, "j2r"] = send(j2s.at[p, :, tail], j2r.at[p, :, tail], up)

    def row_grads(p):
        row_left(p)
        send_left(p)
        row_right(p)
        send_right(p)

    def merge(p):
        back[p, "ol"].wait_recv()
        j2s[p, :, 0:HALF] = (rgf[p % 2, 32:48, 0:HALF] + o3r[p, :, 0:HALF].astype(F32)).astype(BF16)
        back[p, "j2l"] = send(j2s.at[p, :, left], j2r.at[p, :, left], up)
        back[p, "or"].wait_recv()
        j1s[p, :, HALF:D] = (rgf[p % 2, 16:32, HALF:D] + o3r[p, :, HALF:D].astype(F32)).astype(BF16)
        j1s[p, :, D:] = hi_lo(rgf[p % 2, 16:32, D:] + from_hi_lo(o3r[p, :, D:]))
        back[p, "j1r"] = send(j1s.at[p, :, tail], j1r.at[p, :, tail], down)

    def home(p):
        for part in ("j1l", "j1r", "j2l", "j2r"):
            back[p, part].wait_recv()
        for q in range(4):
            cols = slice(q * QUART, (q + 1) * QUART)
            full = rgf[p % 2, 0:16, cols] + j1r[p, :, cols].astype(F32) + j2r[p, :, cols].astype(F32)
            fstk[16 * q:16 * q + 16, 0:QUART] = full.astype(BF16)
        total = hi_lo(rgf[p % 2, 0:16, D:] + from_hi_lo(j1r[p, :, D:]) + from_hi_lo(j2r[p, :, D:]))
        for q in range(4):
            fstk[16 * q:16 * q + 16, QUART:] = total
        block = jnp.dot(perm[...], fstk[...], preferred_element_type=F32).astype(BF16)
        rets[64 * p:64 * p + 64, :] = block
        if p == 0:
            retr[0:16, :] = block[0:16]
        for k in range(4 * p, 4 * p + 4):
            if k:
                part = pl.ds(16 * k, 16)
                back[k] = send(rets.at[part], retr.at[part], source(k))

    def weight_grads(lo, hi):
        @pl.loop(lo, hi)
        def _(t):
            cols = pl.ds(pl.multiple_of(t * 512, 512), 512)
            both = jnp.dot(dlt[...], xg[0, :, cols], preferred_element_type=F32)
            ggo[cols, :] = both[0:FFD].T.astype(BF16)
            guo[cols, :] = both[FFD:].T.astype(BF16)
            gdo[:, cols] = jnp.dot(hidt[...], xg[1, :, cols], preferred_element_type=F32).astype(BF16)

    send_part(2)
    rest(0)
    pick_rows(1, og, 64, TOK)
    send_part(3)
    rest(1)
    ld_wg.wait()
    ld_wu.wait()
    ld_wd.wait()
    forward(0)
    spread(2)
    send_part(4)
    forward(1)
    opposite(0)
    spread(3)
    send_part(5)
    weights = send(wgu, wgup, other)
    forward(2)
    opposite(1)
    project(0)
    compute(0)
    spread(4)
    send_part(6)
    forward(3)
    opposite(2)
    spread(5)
    send_part(7)
    weights.wait_recv()
    row_grads(0)
    forward(4)
    opposite(3)
    project(1)
    compute(1)
    spread(6)
    merge(0)
    forward(5)
    opposite(4)
    spread(7)
    row_grads(1)
    home(0)
    forward(6)
    opposite(5)
    project(2)
    compute(2)
    forward(7)
    opposite(6)
    row_left(2)
    row_right(2)
    project(3)
    merge(1)
    opposite(7)
    send_left(2)
    send_right(2)
    compute(3)
    home(1)
    row_left(3)
    send_left(3)
    row_right(3)
    send_right(3)
    merge(2)
    home(2)
    merge(3)
    weight_grads(0, 14)
    home(3)
    for k in range(1, NODES):
        back[k].wait_recv()
    for copy in remote:
        copy.wait_send()


def scatter_kernel(ids, gates, ret, grad_hbm, gate_grad, grad, sem):
    copies = []

    def start(src, dst):
        copy = pltpu.make_async_copy(src, dst, sem.at[len(copies)])
        copies.append(copy)
        copy.start()

    node = lax.axis_index("node")
    gx, gz = node // SIDE, node % SIDE
    target, gate = slot_targets(ids[...], gates[...])
    eye = iota((TOK, TOK), 0) == iota((TOK, TOK), 1)
    target_col = jnp.sum(jnp.where(eye, target, 0.0), axis=1, keepdims=True)
    want, quarter = wanted(iota((TOK, TOK), 1), gx, gz)
    hit = want == target_col
    for q in range(4):
        chosen = jnp.where(hit & (quarter == q), 1.0, 0.0).astype(BF16)
        cols = pl.ds(q * QUART, QUART)
        grad[:, cols] = jnp.dot(chosen, ret[:, 0:QUART], preferred_element_type=F32).astype(BF16)
        start(grad.at[:, cols], grad_hbm.at[:, cols])
        if q == 0:
            pair = jnp.dot(chosen, ret[:, QUART:], preferred_element_type=F32)
            total = jnp.sum(jnp.where((iota(pair.shape, 1) & 63) == 0, pair, 0.0), axis=1, keepdims=True)
            total = jnp.sum(jnp.where(eye, total, 0.0), axis=0, keepdims=True)
            scaled = total / jnp.where(gate > 0.0, gate, 1.0)
            gate_grad[...] = jnp.where(ids[...] < NODES, scaled, 0.0)
    for copy in copies:
        copy.wait()


def body(tokens, out_grad, route_ids, route_gates, w_gate, w_up, w_down):
    any_space = pl.BlockSpec(memory_space=pl.ANY)
    in_vmem = pl.BlockSpec(memory_space=pltpu.VMEM)
    ids, gates = route_ids.T, route_gates.T
    copies = 30 + 8 * 7 + 6 + 4 + 4 * 6 + 15 + 1
    ret, gg, gu, gd = pl.pallas_call(
        exchange_kernel,
        out_shape=(
            pltpu.VMEM((TOK, QUART + SCW), BF16),
            pltpu.VMEM((D, FFD), BF16),
            pltpu.VMEM((D, FFD), BF16),
            pltpu.VMEM((FFD, D), BF16),
        ),
        in_specs=[any_space] * 7,
        out_specs=(in_vmem,) * 4,
        scratch_shapes=[
            pltpu.VMEM((8, TOK), jnp.int32),
            pltpu.VMEM((8, TOK), BF16),
            pltpu.VMEM((TOK, D), BF16),
            pltpu.VMEM((TOK, D), BF16),
            pltpu.VMEM((8, TOK, TOK), BF16),
            pltpu.VMEM((2, TOK, QUART), BF16),
            pltpu.VMEM((2, TOK, QUART), BF16),
            pltpu.VMEM((2, 8, 64, QUART), BF16),
            pltpu.VMEM((2, PH * ROWS, D), BF16),
            pltpu.VMEM((D, 2 * FFD), BF16),
            pltpu.VMEM((D, 2 * FFD), BF16),
            pltpu.VMEM((FFD, D), BF16),
            pltpu.VMEM((PH, 64, 2 * FFD), BF16),
            pltpu.VMEM((2 * FFD, PH * ROWS), BF16),
            pltpu.VMEM((FFD, PH * ROWS), BF16),
            pltpu.VMEM((PH, 64, SCW), F32),
            pltpu.VMEM((PH, 64, 2 * FFD + SCW), BF16),
            pltpu.VMEM((PH, 64, 2 * FFD + SCW), BF16),
            pltpu.VMEM((2, 48, RW), F32),
            pltpu.VMEM((PH, 16, RW), BF16),
            pltpu.VMEM((PH, 16, RW), BF16),
            pltpu.VMEM((PH, 16, RW), BF16),
            pltpu.VMEM((PH, 16, RW), BF16),
            pltpu.VMEM((PH, 16, RW), BF16),
            pltpu.VMEM((PH, 16, RW), BF16),
            pltpu.VMEM((64, QUART + SCW), BF16),
            pltpu.VMEM((TOK, QUART + SCW), BF16),
            pltpu.VMEM((64, 64), BF16),
            pltpu.VMEM((ROWS, 2 * FFD), F32),
            pltpu.SemaphoreType.DMA((copies,)),
            pltpu.SemaphoreType.DMA((copies,)),
            pltpu.SemaphoreType.DMA((9,)),
        ],
        compiler_params=pltpu.CompilerParams(
            collective_id=0, has_side_effects=True, vmem_limit_bytes=50 * 2**20
        ),
        cost_estimate=pl.CostEstimate(
            flops=8 * 10**9, bytes_accessed=20 * 10**6, transcendentals=65536
        ),
        name="exchange",
    )(ids, gates, tokens, out_grad, w_gate[0], w_up[0], w_down[0])
    token_grad, gate_grad = pl.pallas_call(
        scatter_kernel,
        out_shape=(
            jax.ShapeDtypeStruct((TOK, D), BF16),
            jax.ShapeDtypeStruct((8, TOK), F32),
        ),
        in_specs=[in_vmem] * 3,
        out_specs=(any_space, in_vmem),
        scratch_shapes=[
            pltpu.VMEM((TOK, D), BF16),
            pltpu.SemaphoreType.DMA((4,)),
        ],
        compiler_params=pltpu.CompilerParams(vmem_limit_bytes=16 * 2**20),
        name="scatter",
    )(ids, gates, pltpu.with_memory_space_constraint(ret, pltpu.VMEM))
    return token_grad, gate_grad.T, gg[None], gu[None], gd[None]


def solution(mesh):
    return jax.shard_map(
        body,
        mesh=mesh,
        in_specs=(
            P(("node", "local"), None),
            P(("node", "local"), None),
            P(("node", "local"), None),
            P(("node", "local"), None),
            P("node", None, "local"),
            P("node", None, "local"),
            P("node", "local", None),
        ),
        out_specs=(
            P(("node", "local"), None),
            P(("node", "local"), None),
            P("node", None, "local"),
            P("node", None, "local"),
            P("node", "local", None),
        ),
        check_vma=False,
    )
```

```python
import functools

import jax
import jax.numpy as jnp
from jax import lax
from jax.experimental import pallas as pl
from jax.experimental.pallas import tpu as pltpu
from jax.sharding import PartitionSpec as P

MESH = pl.DeviceIdType.MESH
F32 = jnp.float32
BF16 = jnp.bfloat16

CAP = 4
TOK = 256
D = 7168
HALF = D // 2
QUART = D // 4
FFD = 128
NODES = 16
SIDE = 4
SCW = 128
RW = D + SCW
PH = 4
OFFSETS = (
    (0, 0), (1, 1), (3, 3), (1, 3), (3, 1), (0, 2), (2, 0), (2, 2),
    (1, 2), (3, 2), (2, 1), (2, 3), (0, 1), (0, 3), (1, 0), (3, 0),
)


def two_bits(values):
    word = sum(v << (2 * i) for i, v in enumerate(values))
    return word - 2**32 if word >= 2**31 else word


DX_BITS = two_bits([dx for dx, _ in OFFSETS])
DZ_BITS = two_bits([dz for _, dz in OFFSETS])
ROWS = 128


def iota(shape, dim):
    return lax.broadcasted_iota(jnp.int32, shape, dim)


def slot_targets(ids, gates):
    held = ids < NODES
    expert = jnp.sum(jnp.where(held, ids, 0).astype(F32), axis=0, keepdims=True)
    inside = jnp.sum(jnp.where(held, 1.0, 0.0), axis=0, keepdims=True) > 0.5
    gate = jnp.sum(jnp.where(held, gates.astype(F32), 0.0), axis=0, keepdims=True)
    row = iota((NODES, TOK), 0).astype(F32)
    one_hot = jnp.where((row == expert) & inside, 1.0, 0.0)
    before = jnp.where(iota((TOK, TOK), 0) < iota((TOK, TOK), 1), 1.0, 0.0)
    ranks = jnp.dot(one_hot.astype(BF16), before.astype(BF16), preferred_element_type=F32)
    rank = jnp.sum(ranks * one_hot, axis=0, keepdims=True)
    target = jnp.where(inside, expert * CAP + rank, -1.0)
    return target, gate


def wanted(block, gx, gz):
    k = block >> 4
    dx = lax.shift_right_logical(jnp.full(k.shape, DX_BITS, jnp.int32), 2 * k) & 3
    dz = lax.shift_right_logical(jnp.full(k.shape, DZ_BITS, jnp.int32), 2 * k) & 3
    node = ((gx - dx) & 3) * SIDE + ((gz - dz) & 3)
    return (node * CAP + (block & 3)).astype(F32), (block >> 2) & 3


def hi_lo(score):
    hi = score.astype(BF16).astype(F32)
    lane = iota(score.shape, 1)
    return jnp.where(lane < 64, hi, score - hi).astype(BF16)


def from_hi_lo(pair):
    wide = pair.astype(F32)
    return wide + pltpu.roll(wide, 64, 1)


def contract_cols(left, right):
    return lax.dot_general(left, right, (((1,), (1,)), ((), ())), preferred_element_type=F32)


def exchange_kernel(
    ids_hbm, gates_hbm, tok_hbm, og_hbm, wg_hbm, wu_hbm, wd_hbm,
    retr, ggo, guo, gdo,
    ids, gates, tok, og, pick, sraw, rraw, rx, xg, wgu, wgup, wd,
    dl, dlt, hidt, score, psend, precv,
    rgf, o3s, o3r, j1s, j1r, j2s, j2r, fstk, rets, perm, pre_ref,
    ssem, rsem, lsem,
):
    node = lax.axis_index("node")
    loc = lax.axis_index("local")
    gx, gz = node // SIDE, node % SIDE
    y, c = loc // 2, loc % 2
    up = (node, ((y + 1) % 4) * 2 + c)
    down = (node, ((y + 3) % 4) * 2 + c)
    other = (node, y * 2 + 1 - c)

    def dest(k):
        dx, dz = OFFSETS[k]
        return (((gx + 4 - dx) % 4) * SIDE + (gz + 4 - dz) % 4, loc)

    def source(k):
        dx, dz = OFFSETS[k]
        return (((gx + dx) % 4) * SIDE + (gz + dz) % 4, loc)

    barrier = pltpu.get_barrier_semaphore()
    partners = [up, down, other] + [dest(k) for k in range(1, NODES)]
    for who in partners:
        pl.semaphore_signal(barrier, inc=1, device_id=who, device_id_type=MESH)

    local = []

    def load(src, dst):
        copy = pltpu.make_async_copy(src, dst, lsem.at[len(local)])
        local.append(copy)
        copy.start()
        return copy

    ld_ids = load(ids_hbm, ids)
    ld_gates = load(gates_hbm, gates)
    ld_tok = load(tok_hbm, tok)

    remote = []

    def send(src, dst, who):
        i = len(remote)
        copy = pltpu.make_async_remote_copy(
            src_ref=src, dst_ref=dst, send_sem=ssem.at[i], recv_sem=rsem.at[i],
            device_id=who, device_id_type=MESH,
        )
        remote.append(copy)
        copy.start()
        return copy

    ld_ids.wait()
    ld_gates.wait()
    target, gate = slot_targets(ids[...], gates[...])
    want, quarter = wanted(iota((TOK, TOK), 0), gx, gz)
    hit = want == target
    for q in range(4):
        chosen = hit & (quarter == q)
        pick[q] = jnp.where(chosen, 1.0, 0.0).astype(BF16)
        pick[4 + q] = jnp.where(chosen, gate, 0.0).astype(BF16)
    pi, pj = iota((64, 64), 0), iota((64, 64), 1)
    swapped = ((pj >> 2) & 3) * 16 + (pj >> 4) * 4 + (pj & 3)
    perm[...] = jnp.where(pi == swapped, 1.0, 0.0).astype(BF16)

    def pick_rows(a, rows, lo, hi):
        @pl.loop(0, QUART // 256)
        def _(t):
            acc = jnp.zeros((hi - lo, 256), F32)
            for q in range(4):
                cols = pl.ds(pl.multiple_of(q * QUART + t * 256, 256), 256)
                acc += jnp.dot(pick[4 * a + q, lo:hi, :], rows[:, cols], preferred_element_type=F32)
            cols = pl.ds(pl.multiple_of(t * 256, 256), 256)
            sraw[a, lo:hi, cols] = acc.astype(BF16)
            if lo == 0:
                rx[a, 0, 0:16, cols] = acc[0:16].astype(BF16)

    scatter = {}

    def send_part(u):
        a, p = u % 2, u // 2
        for k in range(4 * p, 4 * p + 4):
            if k:
                part = pl.ds(16 * k, 16)
                land = rraw.at[a, part] if p else rx.at[a, 0, part]
                scatter[a, k] = send(sraw.at[a, part], land, dest(k))

    gath = {}

    def own_block(a, name, rows):
        block = rx.at[a, 0, rows]
        gath[a, "u" + name] = send(block, rx.at[a, 1, rows], up)
        gath[a, "d" + name] = send(block, rx.at[a, 2, rows], down)
        gath[a, "c0" + name] = send(block, rx.at[a, 4, rows], other)

    def rest(a):
        for k in range(1, 4):
            scatter[a, k].wait_recv()
        own_block(a, "", pl.ds(16, 48))

    ld_tok.wait()
    ld_og = load(og_hbm, og)
    pick_rows(0, tok, 0, 64)
    pl.semaphore_wait(barrier, len(partners))
    own_block(0, "first", pl.ds(0, 16))
    send_part(0)
    ld_og.wait()
    ld_wg = load(wg_hbm, wgu.at[:, pl.ds(0, FFD)])
    ld_wu = load(wu_hbm, wgu.at[:, pl.ds(FFD, FFD)])
    ld_wd = load(wd_hbm, wd)
    pick_rows(1, og, 0, 64)
    own_block(1, "first", pl.ds(0, 16))
    send_part(1)
    pick_rows(0, tok, 64, TOK)

    left, right = pl.ds(0, HALF), pl.ds(HALF, HALF)

    def unit(u):
        return u % 2, (u // 2) * ROWS

    def spread(u):
        a, at = unit(u)
        p = u // 2
        for k in range(4 * p, 4 * p + 4):
            if k:
                scatter[a, k].wait_recv()
        rows = jnp.dot(perm[...], rraw[a, 64 * p:64 * p + 64, :], preferred_element_type=F32).astype(BF16)
        for q in range(4):
            xg[a, at:at + 16, q * QUART:(q + 1) * QUART] = rows[16 * q:16 * q + 16]
        mine = xg.at[a, pl.ds(at, 16)]
        gath[u, "u"] = send(mine, xg.at[a, pl.ds(at + 16, 16)], up)
        gath[u, "d"] = send(mine, xg.at[a, pl.ds(at + 32, 16)], down)
        gath[u, "c0"] = send(mine, xg.at[a, pl.ds(at + 64, 16)], other)

    def forward(u):
        a, at = unit(u)
        if u < 2:
            near, far = pl.ds(0, QUART // 2), pl.ds(QUART // 2, QUART // 2)
            gath[u, "ufirst"].wait_recv()
            gath[u, "u"].wait_recv()
            gath[u, "fu"] = send(rx.at[a, 1, :, near], rx.at[a, 3, :, near], up)
            gath[u, "dfirst"].wait_recv()
            gath[u, "d"].wait_recv()
            gath[u, "fd"] = send(rx.at[a, 2, :, far], rx.at[a, 3, :, far], down)
            gath[u, "c12"] = send(rx.at[a, pl.ds(1, 2)], rx.at[a, pl.ds(5, 2)], other)
            return
        opp = pl.ds(at + 48, 16)
        gath[u, "u"].wait_recv()
        gath[u, "fu"] = send(xg.at[a, pl.ds(at + 16, 16), left], xg.at[a, opp, left], up)
        gath[u, "d"].wait_recv()
        gath[u, "fd"] = send(xg.at[a, pl.ds(at + 32, 16), right], xg.at[a, opp, right], down)
        gath[u, "c12"] = send(xg.at[a, pl.ds(at + 16, 32)], xg.at[a, pl.ds(at + 80, 32)], other)

    def opposite(u):
        a, at = unit(u)
        gath[u, "fu"].wait_recv()
        gath[u, "fd"].wait_recv()
        if u < 2:
            gath[u, "c3"] = send(rx.at[a, 3], rx.at[a, 7], other)
            return
        gath[u, "c3"] = send(xg.at[a, pl.ds(at + 48, 16)], xg.at[a, pl.ds(at + 112, 16)], other)

    back = {}

    def arrived(u):
        a, at = unit(u)
        for part in ("c0", "c12", "c3"):
            gath[u, part].wait_recv()
        if u < 2:
            gath[u, "c0first"].wait_recv()

            @pl.loop(0, 8)
            def _(b):
                rows = jnp.dot(perm[...], rx[a, b], preferred_element_type=F32).astype(BF16)
                to = pl.ds(pl.multiple_of(b * 16, 16), 16)
                for q in range(4):
                    xg[a, to, q * QUART:(q + 1) * QUART] = rows[16 * q:16 * q + 16]

    def project(p):
        arrived(2 * p)
        at = p * ROWS
        pre_ref[...] = jnp.dot(xg[0, at:at + ROWS, :], wgu[...], preferred_element_type=F32)

    def compute(p):
        arrived(2 * p + 1)
        at = p * ROWS
        pre = pre_ref[...]
        hidden_grad = contract_cols(xg[1, at:at + ROWS, :], wd[...])
        gate_pre, up_pre = pre[:, :FFD], pre[:, FFD:]
        logistic = jax.nn.sigmoid(gate_pre)
        silu = gate_pre * logistic
        hidden = (silu * up_pre).astype(BF16).astype(F32)
        gate_delta = hidden_grad * up_pre * logistic * (1.0 + gate_pre * (1.0 - logistic))
        up_delta = hidden_grad * silu
        part = jnp.sum(hidden * hidden_grad, axis=1, keepdims=True)
        part = jnp.broadcast_to(part, (ROWS, SCW))
        psend[p, :, 0:FFD] = gate_delta[64:128].astype(BF16)
        psend[p, :, FFD:2 * FFD] = up_delta[64:128].astype(BF16)
        psend[p, :, 2 * FFD:] = hi_lo(part[64:128])
        back[p, "c"] = send(psend.at[p], precv.at[p], other)
        score[p] = part[0:64]
        dl[p, :, 0:FFD] = gate_delta[0:64].astype(BF16)
        dl[p, :, FFD:2 * FFD] = up_delta[0:64].astype(BF16)
        dlt[0:FFD, at:at + ROWS] = gate_delta.T.astype(BF16)
        dlt[FFD:2 * FFD, at:at + ROWS] = up_delta.T.astype(BF16)
        hidt[:, at:at + ROWS] = hidden.T.astype(BF16)

    tail = pl.ds(HALF, RW - HALF)

    def row_tiles(p, lo, hi, ready):
        mine, theirs = dl[p], precv[p, :, 0:2 * FFD]

        @pl.loop(lo, hi)
        def _(t):
            cols = pl.ds(pl.multiple_of(t * 512, 512), 512)
            grad = contract_cols(mine, wgu[cols, :]) + contract_cols(theirs, wgup[cols, :])
            rgf[p % 3, :, cols] = grad[0:48]
            o3s[p, :, cols] = grad[48:64].astype(BF16)
            ready[p, :, cols] = grad[16:32].astype(BF16) if ready is j1s else grad[32:48].astype(BF16)

    def row_left(p):
        back[p, "c"].wait_recv()
        total = score[p] + from_hi_lo(precv[p, :, 2 * FFD:])
        rgf[p % 3, :, D:] = total[0:48]
        o3s[p, :, D:] = hi_lo(total[48:64])
        j2s[p, :, D:] = hi_lo(total[32:48])
        row_tiles(p, 0, 7, j1s)

    def row_right(p):
        row_tiles(p, 7, 14, j2s)

    def send_left(p):
        back[p, "ol"] = send(o3s.at[p, :, left], o3r.at[p, :, left], up)
        back[p, "j1l"] = send(j1s.at[p, :, left], j1r.at[p, :, left], down)

    def send_right(p):
        back[p, "or"] = send(o3s.at[p, :, tail], o3r.at[p, :, tail], down)
        back[p, "j2r"] = send(j2s.at[p, :, tail], j2r.at[p, :, tail], up)

    def row_grads(p):
        row_left(p)
        send_left(p)
        row_right(p)
        send_right(p)

    def merge(p):
        back[p, "ol"].wait_recv()
        j2s[p, :, 0:HALF] = (rgf[p % 3, 32:48, 0:HALF] + o3r[p, :, 0:HALF].astype(F32)).astype(BF16)
        back[p, "j2l"] = send(j2s.at[p, :, left], j2r.at[p, :, left], up)
        back[p, "or"].wait_recv()
        j1s[p, :, HALF:D] = (rgf[p % 3, 16:32, HALF:D] + o3r[p, :, HALF:D].astype(F32)).astype(BF16)
        j1s[p, :, D:] = hi_lo(rgf[p % 3, 16:32, D:] + from_hi_lo(o3r[p, :, D:]))
        back[p, "j1r"] = send(j1s.at[p, :, tail], j1r.at[p, :, tail], down)

    def home(p):
        for part in ("j1l", "j1r", "j2l", "j2r"):
            back[p, part].wait_recv()
        for q in range(4):
            cols = slice(q * QUART, (q + 1) * QUART)
            full = rgf[p % 3, 0:16, cols] + j1r[p, :, cols].astype(F32) + j2r[p, :, cols].astype(F32)
            fstk[16 * q:16 * q + 16, 0:QUART] = full.astype(BF16)
        total = hi_lo(rgf[p % 3, 0:16, D:] + from_hi_lo(j1r[p, :, D:]) + from_hi_lo(j2r[p, :, D:]))
        for q in range(4):
            fstk[16 * q:16 * q + 16, QUART:] = total
        block = jnp.dot(perm[...], fstk[...], preferred_element_type=F32).astype(BF16)
        rets[64 * p:64 * p + 64, :] = block
        if p == 0:
            retr[0:16, :] = block[0:16]
        for k in range(4 * p, 4 * p + 4):
            if k:
                part = pl.ds(16 * k, 16)
                back[k] = send(rets.at[part], retr.at[part], source(k))

    def half_quarter(q, piece, score):
        at = q * QUART + piece * (QUART // 2)
        return slice(at, at + QUART // 2 + (SCW if score else 0))

    def merge_pieces(p):
        for piece in range(2):
            if piece == 0:
                back[p, "ol"].wait_recv()
            for q in range(2):
                cols = half_quarter(q, piece, False)
                j2s[p, :, cols] = (rgf[p % 3, 32:48, cols] + o3r[p, :, cols].astype(F32)).astype(BF16)
                back[p, "j2l", piece, q] = send(j2s.at[p, :, cols], j2r.at[p, :, cols], up)
            if piece == 0:
                back[p, "or"].wait_recv()
            for q in range(2, 4):
                cols = half_quarter(q, piece, False)
                j1s[p, :, cols] = (rgf[p % 3, 16:32, cols] + o3r[p, :, cols].astype(F32)).astype(BF16)
                score_too = piece == 1 and q == 3
                if score_too:
                    j1s[p, :, D:] = hi_lo(rgf[p % 3, 16:32, D:] + from_hi_lo(o3r[p, :, D:]))
                cols = half_quarter(q, piece, score_too)
                back[p, "j1r", piece, q] = send(j1s.at[p, :, cols], j1r.at[p, :, cols], down)

    def home_piece(p, piece):
        if piece == 0:
            back[p, "j1l"].wait_recv()
            back[p, "j2r"].wait_recv()
        for q in range(4):
            back[(p, "j2l", piece, q) if q < 2 else (p, "j1r", piece, q)].wait_recv()
            cols = half_quarter(q, piece, False)
            full = rgf[p % 3, 0:16, cols] + j1r[p, :, cols].astype(F32) + j2r[p, :, cols].astype(F32)
            fstk[16 * q:16 * q + 16, half_quarter(0, piece, False)] = full.astype(BF16)
        if piece == 1:
            total = hi_lo(rgf[p % 3, 0:16, D:] + from_hi_lo(j1r[p, :, D:]) + from_hi_lo(j2r[p, :, D:]))
            for q in range(4):
                fstk[16 * q:16 * q + 16, QUART:] = total
        cols = half_quarter(0, piece, piece == 1)
        block = jnp.dot(perm[...], fstk[:, cols], preferred_element_type=F32).astype(BF16)
        rets[64 * p:64 * p + 64, cols] = block
        for k in range(4 * p, 4 * p + 4):
            part = pl.ds(16 * k, 16)
            back[k, piece] = send(rets.at[part, cols], retr.at[part, cols], source(k))

    def weight_grads(lo, hi):
        @pl.loop(lo, hi)
        def _(t):
            cols = pl.ds(pl.multiple_of(t * 512, 512), 512)
            both = jnp.dot(dlt[...], xg[0, :, cols], preferred_element_type=F32)
            ggo[cols, :] = both[0:FFD].T.astype(BF16)
            guo[cols, :] = both[FFD:].T.astype(BF16)
            gdo[:, cols] = jnp.dot(hidt[...], xg[1, :, cols], preferred_element_type=F32).astype(BF16)

    send_part(2)
    rest(0)
    pick_rows(1, og, 64, TOK)
    send_part(3)
    rest(1)
    ld_wg.wait()
    ld_wu.wait()
    ld_wd.wait()
    forward(0)
    spread(2)
    send_part(4)
    forward(1)
    opposite(0)
    spread(3)
    send_part(5)
    weights = send(wgu, wgup, other)
    forward(2)
    opposite(1)
    project(0)
    compute(0)
    spread(4)
    send_part(6)
    forward(3)
    opposite(2)
    spread(5)
    send_part(7)
    weights.wait_recv()
    row_grads(0)
    forward(4)
    opposite(3)
    project(1)
    compute(1)
    spread(6)
    merge(0)
    forward(5)
    opposite(4)
    spread(7)
    row_grads(1)
    home(0)
    forward(6)
    opposite(5)
    project(2)
    compute(2)
    forward(7)
    opposite(6)
    row_left(2)
    row_right(2)
    project(3)
    merge(1)
    opposite(7)
    send_left(2)
    send_right(2)
    compute(3)
    merge(2)
    row_left(3)
    send_left(3)
    row_right(3)
    send_right(3)
    home(1)
    home(2)
    merge_pieces(3)
    weight_grads(0, 6)
    home_piece(3, 0)
    home_piece(3, 1)
    weight_grads(6, 14)
    for k in range(1, 12):
        back[k].wait_recv()
    for k in range(12, NODES):
        back[k, 0].wait_recv()
        back[k, 1].wait_recv()
    for copy in remote:
        copy.wait_send()


def scatter_kernel(ids, gates, ret, grad_hbm, gate_grad, grad, sem):
    copies = []

    def start(src, dst):
        copy = pltpu.make_async_copy(src, dst, sem.at[len(copies)])
        copies.append(copy)
        copy.start()

    node = lax.axis_index("node")
    gx, gz = node // SIDE, node % SIDE
    target, gate = slot_targets(ids[...], gates[...])
    eye = iota((TOK, TOK), 0) == iota((TOK, TOK), 1)
    target_col = jnp.sum(jnp.where(eye, target, 0.0), axis=1, keepdims=True)
    want, quarter = wanted(iota((TOK, TOK), 1), gx, gz)
    hit = want == target_col
    for q in range(4):
        chosen = jnp.where(hit & (quarter == q), 1.0, 0.0).astype(BF16)
        cols = pl.ds(q * QUART, QUART)
        grad[:, cols] = jnp.dot(chosen, ret[:, 0:QUART], preferred_element_type=F32).astype(BF16)
        start(grad.at[:, cols], grad_hbm.at[:, cols])
        if q == 0:
            pair = jnp.dot(chosen, ret[:, QUART:], preferred_element_type=F32)
            total = jnp.sum(jnp.where((iota(pair.shape, 1) & 63) == 0, pair, 0.0), axis=1, keepdims=True)
            total = jnp.sum(jnp.where(eye, total, 0.0), axis=0, keepdims=True)
            scaled = total / jnp.where(gate > 0.0, gate, 1.0)
            gate_grad[...] = jnp.where(ids[...] < NODES, scaled, 0.0)
    for copy in copies:
        copy.wait()


def body(tokens, out_grad, route_ids, route_gates, w_gate, w_up, w_down):
    any_space = pl.BlockSpec(memory_space=pl.ANY)
    in_vmem = pl.BlockSpec(memory_space=pltpu.VMEM)
    ids, gates = route_ids.T, route_gates.T
    copies = 30 + 8 * 7 + 6 + 4 + 4 * 6 + 15 + 1 + 10
    ret, gg, gu, gd = pl.pallas_call(
        exchange_kernel,
        out_shape=(
            pltpu.VMEM((TOK, QUART + SCW), BF16),
            pltpu.VMEM((D, FFD), BF16),
            pltpu.VMEM((D, FFD), BF16),
            pltpu.VMEM((FFD, D), BF16),
        ),
        in_specs=[any_space] * 7,
        out_specs=(in_vmem,) * 4,
        scratch_shapes=[
            pltpu.VMEM((8, TOK), jnp.int32),
            pltpu.VMEM((8, TOK), BF16),
            pltpu.VMEM((TOK, D), BF16),
            pltpu.VMEM((TOK, D), BF16),
            pltpu.VMEM((8, TOK, TOK), BF16),
            pltpu.VMEM((2, TOK, QUART), BF16),
            pltpu.VMEM((2, TOK, QUART), BF16),
            pltpu.VMEM((2, 8, 64, QUART), BF16),
            pltpu.VMEM((2, PH * ROWS, D), BF16),
            pltpu.VMEM((D, 2 * FFD), BF16),
            pltpu.VMEM((D, 2 * FFD), BF16),
            pltpu.VMEM((FFD, D), BF16),
            pltpu.VMEM((PH, 64, 2 * FFD), BF16),
            pltpu.VMEM((2 * FFD, PH * ROWS), BF16),
            pltpu.VMEM((FFD, PH * ROWS), BF16),
            pltpu.VMEM((PH, 64, SCW), F32),
            pltpu.VMEM((PH, 64, 2 * FFD + SCW), BF16),
            pltpu.VMEM((PH, 64, 2 * FFD + SCW), BF16),
            pltpu.VMEM((3, 48, RW), F32),
            pltpu.VMEM((PH, 16, RW), BF16),
            pltpu.VMEM((PH, 16, RW), BF16),
            pltpu.VMEM((PH, 16, RW), BF16),
            pltpu.VMEM((PH, 16, RW), BF16),
            pltpu.VMEM((PH, 16, RW), BF16),
            pltpu.VMEM((PH, 16, RW), BF16),
            pltpu.VMEM((64, QUART + SCW), BF16),
            pltpu.VMEM((TOK, QUART + SCW), BF16),
            pltpu.VMEM((64, 64), BF16),
            pltpu.VMEM((ROWS, 2 * FFD), F32),
            pltpu.SemaphoreType.DMA((copies,)),
            pltpu.SemaphoreType.DMA((copies,)),
            pltpu.SemaphoreType.DMA((9,)),
        ],
        compiler_params=pltpu.CompilerParams(
            collective_id=0, has_side_effects=True, vmem_limit_bytes=52 * 2**20
        ),
        cost_estimate=pl.CostEstimate(
            flops=8 * 10**9, bytes_accessed=20 * 10**6, transcendentals=65536
        ),
        name="exchange",
    )(ids, gates, tokens, out_grad, w_gate[0], w_up[0], w_down[0])
    token_grad, gate_grad = pl.pallas_call(
        scatter_kernel,
        out_shape=(
            jax.ShapeDtypeStruct((TOK, D), BF16),
            jax.ShapeDtypeStruct((8, TOK), F32),
        ),
        in_specs=[in_vmem] * 3,
        out_specs=(any_space, in_vmem),
        scratch_shapes=[
            pltpu.VMEM((TOK, D), BF16),
            pltpu.SemaphoreType.DMA((4,)),
        ],
        compiler_params=pltpu.CompilerParams(vmem_limit_bytes=16 * 2**20),
        name="scatter",
    )(ids, gates, pltpu.with_memory_space_constraint(ret, pltpu.VMEM))
    return token_grad, gate_grad.T, gg[None], gu[None], gd[None]


def solution(mesh):
    return jax.shard_map(
        body,
        mesh=mesh,
        in_specs=(
            P(("node", "local"), None),
            P(("node", "local"), None),
            P(("node", "local"), None),
            P(("node", "local"), None),
            P("node", None, "local"),
            P("node", None, "local"),
            P("node", "local", None),
        ),
        out_specs=(
            P(("node", "local"), None),
            P(("node", "local"), None),
            P("node", None, "local"),
            P("node", None, "local"),
            P("node", "local", None),
        ),
        check_vma=False,
    )
```

```python
import functools

import jax
import jax.numpy as jnp
from jax import lax
from jax.experimental import pallas as pl
from jax.experimental.pallas import tpu as pltpu
from jax.sharding import PartitionSpec as P

MESH = pl.DeviceIdType.MESH
F32 = jnp.float32
BF16 = jnp.bfloat16

CAP = 4
TOK = 256
D = 7168
HALF = D // 2
QUART = D // 4
FFD = 128
NODES = 16
SIDE = 4
SCW = 128
RW = D + SCW
PH = 4
OFFSETS = (
    (0, 0), (1, 1), (3, 3), (1, 3), (3, 1), (0, 2), (2, 0), (2, 2),
    (1, 2), (3, 2), (2, 1), (2, 3), (0, 1), (0, 3), (1, 0), (3, 0),
)


def two_bits(values):
    word = sum(v << (2 * i) for i, v in enumerate(values))
    return word - 2**32 if word >= 2**31 else word


DX_BITS = two_bits([dx for dx, _ in OFFSETS])
DZ_BITS = two_bits([dz for _, dz in OFFSETS])
ROWS = 128


def iota(shape, dim):
    return lax.broadcasted_iota(jnp.int32, shape, dim)


def slot_targets(ids, gates):
    held = ids < NODES
    expert = jnp.sum(jnp.where(held, ids, 0).astype(F32), axis=0, keepdims=True)
    inside = jnp.sum(jnp.where(held, 1.0, 0.0), axis=0, keepdims=True) > 0.5
    gate = jnp.sum(jnp.where(held, gates.astype(F32), 0.0), axis=0, keepdims=True)
    row = iota((NODES, TOK), 0).astype(F32)
    one_hot = jnp.where((row == expert) & inside, 1.0, 0.0)
    before = jnp.where(iota((TOK, TOK), 0) < iota((TOK, TOK), 1), 1.0, 0.0)
    ranks = jnp.dot(one_hot.astype(BF16), before.astype(BF16), preferred_element_type=F32)
    rank = jnp.sum(ranks * one_hot, axis=0, keepdims=True)
    target = jnp.where(inside, expert * CAP + rank, -1.0)
    return target, gate


def wanted(block, gx, gz):
    k = block >> 4
    dx = lax.shift_right_logical(jnp.full(k.shape, DX_BITS, jnp.int32), 2 * k) & 3
    dz = lax.shift_right_logical(jnp.full(k.shape, DZ_BITS, jnp.int32), 2 * k) & 3
    node = ((gx - dx) & 3) * SIDE + ((gz - dz) & 3)
    return (node * CAP + (block & 3)).astype(F32), (block >> 2) & 3


def hi_lo(score):
    hi = score.astype(BF16).astype(F32)
    lane = iota(score.shape, 1)
    return jnp.where(lane < 64, hi, score - hi).astype(BF16)


def from_hi_lo(pair):
    wide = pair.astype(F32)
    return wide + pltpu.roll(wide, 64, 1)


def contract_cols(left, right):
    return lax.dot_general(left, right, (((1,), (1,)), ((), ())), preferred_element_type=F32)


def exchange_kernel(
    ids_hbm, gates_hbm, tok_hbm, og_hbm, wg_hbm, wu_hbm, wd_hbm,
    retr, gguo, gdo,
    ids, gates, tok, og, pick, sraw, rraw, rx, xg, wgu, wgup, wd,
    dl, dlt, hidt, score, psend, precv,
    rgf, o3s, o3r, j1s, j1r, j2s, j2r, fstk, rets, perm, pre_ref,
    ssem, rsem, lsem,
):
    node = lax.axis_index("node")
    loc = lax.axis_index("local")
    gx, gz = node // SIDE, node % SIDE
    y, c = loc // 2, loc % 2
    up = (node, ((y + 1) % 4) * 2 + c)
    down = (node, ((y + 3) % 4) * 2 + c)
    other = (node, y * 2 + 1 - c)

    def dest(k):
        dx, dz = OFFSETS[k]
        return (((gx + 4 - dx) % 4) * SIDE + (gz + 4 - dz) % 4, loc)

    def source(k):
        dx, dz = OFFSETS[k]
        return (((gx + dx) % 4) * SIDE + (gz + dz) % 4, loc)

    barrier = pltpu.get_barrier_semaphore()
    partners = [up, down, other] + [dest(k) for k in range(1, NODES)]
    for who in partners:
        pl.semaphore_signal(barrier, inc=1, device_id=who, device_id_type=MESH)

    local = []

    def load(src, dst):
        copy = pltpu.make_async_copy(src, dst, lsem.at[len(local)])
        local.append(copy)
        copy.start()
        return copy

    ld_ids = load(ids_hbm, ids)
    ld_gates = load(gates_hbm, gates)
    ld_tok = load(tok_hbm, tok)

    remote = []

    def send(src, dst, who):
        i = len(remote)
        copy = pltpu.make_async_remote_copy(
            src_ref=src, dst_ref=dst, send_sem=ssem.at[i], recv_sem=rsem.at[i],
            device_id=who, device_id_type=MESH,
        )
        remote.append(copy)
        copy.start()
        return copy

    ld_ids.wait()
    ld_gates.wait()
    target, gate = slot_targets(ids[...], gates[...])
    want, quarter = wanted(iota((TOK, TOK), 0), gx, gz)
    hit = want == target
    for q in range(4):
        chosen = hit & (quarter == q)
        pick[q] = jnp.where(chosen, 1.0, 0.0).astype(BF16)
        pick[4 + q] = jnp.where(chosen, gate, 0.0).astype(BF16)
    pi, pj = iota((64, 64), 0), iota((64, 64), 1)
    swapped = ((pj >> 2) & 3) * 16 + (pj >> 4) * 4 + (pj & 3)
    perm[...] = jnp.where(pi == swapped, 1.0, 0.0).astype(BF16)

    def pick_rows(a, rows, lo, hi):
        @pl.loop(0, QUART // 256)
        def _(t):
            acc = jnp.zeros((hi - lo, 256), F32)
            for q in range(4):
                cols = pl.ds(pl.multiple_of(q * QUART + t * 256, 256), 256)
                acc += jnp.dot(pick[4 * a + q, lo:hi, :], rows[:, cols], preferred_element_type=F32)
            cols = pl.ds(pl.multiple_of(t * 256, 256), 256)
            sraw[a, lo:hi, cols] = acc.astype(BF16)
            if lo == 0:
                rx[a, 0, 0:16, cols] = acc[0:16].astype(BF16)

    scatter = {}

    def send_part(u):
        a, p = u % 2, u // 2
        for k in range(4 * p, 4 * p + 4):
            if k:
                part = pl.ds(16 * k, 16)
                land = rraw.at[a, part] if p else rx.at[a, 0, part]
                scatter[a, k] = send(sraw.at[a, part], land, dest(k))

    gath = {}

    def own_block(a, name, rows):
        block = rx.at[a, 0, rows]
        gath[a, "u" + name] = send(block, rx.at[a, 1, rows], up)
        gath[a, "d" + name] = send(block, rx.at[a, 2, rows], down)
        gath[a, "c0" + name] = send(block, rx.at[a, 4, rows], other)

    def rest(a):
        for k in range(1, 4):
            scatter[a, k].wait_recv()
        own_block(a, "", pl.ds(16, 48))

    ld_tok.wait()
    ld_og = load(og_hbm, og)
    pick_rows(0, tok, 0, 64)
    pl.semaphore_wait(barrier, len(partners))
    own_block(0, "first", pl.ds(0, 16))
    send_part(0)
    ld_og.wait()
    ld_wg = load(wg_hbm, wgu.at[:, pl.ds(0, FFD)])
    ld_wu = load(wu_hbm, wgu.at[:, pl.ds(FFD, FFD)])
    ld_wd = load(wd_hbm, wd)
    pick_rows(1, og, 0, 64)
    own_block(1, "first", pl.ds(0, 16))
    send_part(1)
    pick_rows(0, tok, 64, TOK)

    left, right = pl.ds(0, HALF), pl.ds(HALF, HALF)

    def unit(u):
        return u % 2, (u // 2) * ROWS

    def spread(u):
        a, at = unit(u)
        p = u // 2
        for k in range(4 * p, 4 * p + 4):
            if k:
                scatter[a, k].wait_recv()
        rows = jnp.dot(perm[...], rraw[a, 64 * p:64 * p + 64, :], preferred_element_type=F32).astype(BF16)
        for q in range(4):
            xg[a, at:at + 16, q * QUART:(q + 1) * QUART] = rows[16 * q:16 * q + 16]
        mine = xg.at[a, pl.ds(at, 16)]
        gath[u, "u"] = send(mine, xg.at[a, pl.ds(at + 16, 16)], up)
        gath[u, "d"] = send(mine, xg.at[a, pl.ds(at + 32, 16)], down)
        gath[u, "c0"] = send(mine, xg.at[a, pl.ds(at + 64, 16)], other)

    def forward(u):
        a, at = unit(u)
        if u < 2:
            near, far = pl.ds(0, QUART // 2), pl.ds(QUART // 2, QUART // 2)
            gath[u, "ufirst"].wait_recv()
            gath[u, "u"].wait_recv()
            gath[u, "fu"] = send(rx.at[a, 1, :, near], rx.at[a, 3, :, near], up)
            gath[u, "dfirst"].wait_recv()
            gath[u, "d"].wait_recv()
            gath[u, "fd"] = send(rx.at[a, 2, :, far], rx.at[a, 3, :, far], down)
            gath[u, "c12"] = send(rx.at[a, pl.ds(1, 2)], rx.at[a, pl.ds(5, 2)], other)
            return
        opp = pl.ds(at + 48, 16)
        gath[u, "u"].wait_recv()
        gath[u, "fu"] = send(xg.at[a, pl.ds(at + 16, 16), left], xg.at[a, opp, left], up)
        gath[u, "d"].wait_recv()
        gath[u, "fd"] = send(xg.at[a, pl.ds(at + 32, 16), right], xg.at[a, opp, right], down)
        gath[u, "c12"] = send(xg.at[a, pl.ds(at + 16, 32)], xg.at[a, pl.ds(at + 80, 32)], other)

    def opposite(u):
        a, at = unit(u)
        gath[u, "fu"].wait_recv()
        gath[u, "fd"].wait_recv()
        if u < 2:
            gath[u, "c3"] = send(rx.at[a, 3], rx.at[a, 7], other)
            return
        gath[u, "c3"] = send(xg.at[a, pl.ds(at + 48, 16)], xg.at[a, pl.ds(at + 112, 16)], other)

    back = {}

    def arrived(u):
        a, at = unit(u)
        for part in ("c0", "c12", "c3"):
            gath[u, part].wait_recv()
        if u < 2:
            gath[u, "c0first"].wait_recv()

            @pl.loop(0, 8)
            def _(b):
                rows = jnp.dot(perm[...], rx[a, b], preferred_element_type=F32).astype(BF16)
                to = pl.ds(pl.multiple_of(b * 16, 16), 16)
                for q in range(4):
                    xg[a, to, q * QUART:(q + 1) * QUART] = rows[16 * q:16 * q + 16]

    def project(p):
        arrived(2 * p)
        at = p * ROWS
        pre_ref[...] = jnp.dot(xg[0, at:at + ROWS, :], wgu[...], preferred_element_type=F32)

    def compute(p):
        arrived(2 * p + 1)
        at = p * ROWS
        pre = pre_ref[...]
        hidden_grad = contract_cols(xg[1, at:at + ROWS, :], wd[...])
        gate_pre, up_pre = pre[:, :FFD], pre[:, FFD:]
        logistic = jax.nn.sigmoid(gate_pre)
        silu = gate_pre * logistic
        hidden = (silu * up_pre).astype(BF16).astype(F32)
        gate_delta = hidden_grad * up_pre * logistic * (1.0 + gate_pre * (1.0 - logistic))
        up_delta = hidden_grad * silu
        part = jnp.sum(hidden * hidden_grad, axis=1, keepdims=True)
        part = jnp.broadcast_to(part, (ROWS, SCW))
        psend[p, :, 0:FFD] = gate_delta[64:128].astype(BF16)
        psend[p, :, FFD:2 * FFD] = up_delta[64:128].astype(BF16)
        psend[p, :, 2 * FFD:] = hi_lo(part[64:128])
        back[p, "c"] = send(psend.at[p], precv.at[p], other)
        score[p] = part[0:64]
        dl[p, :, 0:FFD] = gate_delta[0:64].astype(BF16)
        dl[p, :, FFD:2 * FFD] = up_delta[0:64].astype(BF16)
        dlt[0:FFD, at:at + ROWS] = gate_delta.T.astype(BF16)
        dlt[FFD:2 * FFD, at:at + ROWS] = up_delta.T.astype(BF16)
        hidt[:, at:at + ROWS] = hidden.T.astype(BF16)

    tail = pl.ds(HALF, RW - HALF)

    def row_tiles(p, lo, hi, ready):
        mine, theirs = dl[p], precv[p, :, 0:2 * FFD]

        @pl.loop(lo, hi)
        def _(t):
            cols = pl.ds(pl.multiple_of(t * 512, 512), 512)
            grad = contract_cols(mine, wgu[cols, :]) + contract_cols(theirs, wgup[cols, :])
            rgf[p % 3, :, cols] = grad[0:48]
            o3s[p, :, cols] = grad[48:64].astype(BF16)
            ready[p, :, cols] = grad[16:32].astype(BF16) if ready is j1s else grad[32:48].astype(BF16)

    def row_left(p):
        back[p, "c"].wait_recv()
        total = score[p] + from_hi_lo(precv[p, :, 2 * FFD:])
        rgf[p % 3, :, D:] = total[0:48]
        o3s[p, :, D:] = hi_lo(total[48:64])
        j2s[p, :, D:] = hi_lo(total[32:48])
        row_tiles(p, 0, 7, j1s)

    def row_right(p):
        row_tiles(p, 7, 14, j2s)

    def send_left(p):
        back[p, "ol"] = send(o3s.at[p, :, left], o3r.at[p, :, left], up)
        back[p, "j1l"] = send(j1s.at[p, :, left], j1r.at[p, :, left], down)

    def send_right(p):
        back[p, "or"] = send(o3s.at[p, :, tail], o3r.at[p, :, tail], down)
        back[p, "j2r"] = send(j2s.at[p, :, tail], j2r.at[p, :, tail], up)

    def row_grads(p):
        row_left(p)
        send_left(p)
        row_right(p)
        send_right(p)

    def merge(p):
        back[p, "ol"].wait_recv()
        j2s[p, :, 0:HALF] = (rgf[p % 3, 32:48, 0:HALF] + o3r[p, :, 0:HALF].astype(F32)).astype(BF16)
        back[p, "j2l"] = send(j2s.at[p, :, left], j2r.at[p, :, left], up)
        back[p, "or"].wait_recv()
        j1s[p, :, HALF:D] = (rgf[p % 3, 16:32, HALF:D] + o3r[p, :, HALF:D].astype(F32)).astype(BF16)
        j1s[p, :, D:] = hi_lo(rgf[p % 3, 16:32, D:] + from_hi_lo(o3r[p, :, D:]))
        back[p, "j1r"] = send(j1s.at[p, :, tail], j1r.at[p, :, tail], down)

    def home(p):
        for part in ("j1l", "j1r", "j2l", "j2r"):
            back[p, part].wait_recv()
        for q in range(4):
            cols = slice(q * QUART, (q + 1) * QUART)
            full = rgf[p % 3, 0:16, cols] + j1r[p, :, cols].astype(F32) + j2r[p, :, cols].astype(F32)
            fstk[16 * q:16 * q + 16, 0:QUART] = full.astype(BF16)
        total = hi_lo(rgf[p % 3, 0:16, D:] + from_hi_lo(j1r[p, :, D:]) + from_hi_lo(j2r[p, :, D:]))
        for q in range(4):
            fstk[16 * q:16 * q + 16, QUART:] = total
        block = jnp.dot(perm[...], fstk[...], preferred_element_type=F32).astype(BF16)
        rets[64 * p:64 * p + 64, :] = block
        if p == 0:
            retr[0:16, :] = block[0:16]
        for k in range(4 * p, 4 * p + 4):
            if k:
                part = pl.ds(16 * k, 16)
                back[k] = send(rets.at[part], retr.at[part], source(k))

    def half_quarter(q, piece, score):
        at = q * QUART + piece * (QUART // 2)
        return slice(at, at + QUART // 2 + (SCW if score else 0))

    def merge_pieces(p):
        for piece in range(2):
            if piece == 0:
                back[p, "ol"].wait_recv()
            for q in range(2):
                cols = half_quarter(q, piece, False)
                j2s[p, :, cols] = (rgf[p % 3, 32:48, cols] + o3r[p, :, cols].astype(F32)).astype(BF16)
                back[p, "j2l", piece, q] = send(j2s.at[p, :, cols], j2r.at[p, :, cols], up)
            if piece == 0:
                back[p, "or"].wait_recv()
            for q in range(2, 4):
                cols = half_quarter(q, piece, False)
                j1s[p, :, cols] = (rgf[p % 3, 16:32, cols] + o3r[p, :, cols].astype(F32)).astype(BF16)
                score_too = piece == 1 and q == 3
                if score_too:
                    j1s[p, :, D:] = hi_lo(rgf[p % 3, 16:32, D:] + from_hi_lo(o3r[p, :, D:]))
                cols = half_quarter(q, piece, score_too)
                back[p, "j1r", piece, q] = send(j1s.at[p, :, cols], j1r.at[p, :, cols], down)

    def home_piece(p, piece):
        if piece == 0:
            back[p, "j1l"].wait_recv()
            back[p, "j2r"].wait_recv()
        for q in range(4):
            back[(p, "j2l", piece, q) if q < 2 else (p, "j1r", piece, q)].wait_recv()
            cols = half_quarter(q, piece, False)
            full = rgf[p % 3, 0:16, cols] + j1r[p, :, cols].astype(F32) + j2r[p, :, cols].astype(F32)
            fstk[16 * q:16 * q + 16, half_quarter(0, piece, False)] = full.astype(BF16)
        if piece == 1:
            total = hi_lo(rgf[p % 3, 0:16, D:] + from_hi_lo(j1r[p, :, D:]) + from_hi_lo(j2r[p, :, D:]))
            for q in range(4):
                fstk[16 * q:16 * q + 16, QUART:] = total
        cols = half_quarter(0, piece, piece == 1)
        block = jnp.dot(perm[...], fstk[:, cols], preferred_element_type=F32).astype(BF16)
        rets[64 * p:64 * p + 64, cols] = block
        for k in range(4 * p, 4 * p + 4):
            part = pl.ds(16 * k, 16)
            back[k, piece] = send(rets.at[part, cols], retr.at[part, cols], source(k))

    def weight_grads(lo, hi):
        @pl.loop(lo, hi)
        def _(t):
            cols = pl.ds(pl.multiple_of(t * 512, 512), 512)
            both = jnp.dot(dlt[...], xg[0, :, cols], preferred_element_type=F32)
            gguo[cols, :] = both[0:FFD].T.astype(BF16)
            gguo[pl.ds(pl.multiple_of(D + t * 512, 512), 512), :] = both[FFD:].T.astype(BF16)
            gdo[:, cols] = jnp.dot(hidt[...], xg[1, :, cols], preferred_element_type=F32).astype(BF16)

    send_part(2)
    rest(0)
    pick_rows(1, og, 64, TOK)
    send_part(3)
    rest(1)
    ld_wg.wait()
    ld_wu.wait()
    ld_wd.wait()
    forward(0)
    spread(2)
    send_part(4)
    forward(1)
    opposite(0)
    spread(3)
    send_part(5)
    weights = send(wgu, wgup, other)
    forward(2)
    opposite(1)
    project(0)
    compute(0)
    spread(4)
    send_part(6)
    forward(3)
    opposite(2)
    spread(5)
    send_part(7)
    weights.wait_recv()
    row_grads(0)
    forward(4)
    opposite(3)
    project(1)
    compute(1)
    spread(6)
    merge(0)
    forward(5)
    opposite(4)
    spread(7)
    row_grads(1)
    home(0)
    forward(6)
    opposite(5)
    project(2)
    compute(2)
    forward(7)
    opposite(6)
    row_left(2)
    row_right(2)
    project(3)
    merge(1)
    opposite(7)
    send_left(2)
    send_right(2)
    compute(3)
    merge(2)
    row_left(3)
    send_left(3)
    row_right(3)
    send_right(3)
    home(1)
    home(2)
    merge_pieces(3)
    weight_grads(0, 6)
    home_piece(3, 0)
    home_piece(3, 1)
    weight_grads(6, 14)
    for k in range(1, 12):
        back[k].wait_recv()
    for k in range(12, NODES):
        back[k, 0].wait_recv()
        back[k, 1].wait_recv()
    for copy in remote:
        copy.wait_send()


def scatter_kernel(ids, gates, ret, ggu, gd_in, grad_hbm, gate_grad, gg, gu, gd, grad, sem):
    copies = []

    def start(src, dst):
        copy = pltpu.make_async_copy(src, dst, sem.at[len(copies)])
        copies.append(copy)
        copy.start()

    start(ggu.at[pl.ds(0, D)], gg)
    start(ggu.at[pl.ds(D, D)], gu)
    start(gd_in, gd)
    node = lax.axis_index("node")
    gx, gz = node // SIDE, node % SIDE
    target, gate = slot_targets(ids[...], gates[...])
    eye = iota((TOK, TOK), 0) == iota((TOK, TOK), 1)
    target_col = jnp.sum(jnp.where(eye, target, 0.0), axis=1, keepdims=True)
    want, quarter = wanted(iota((TOK, TOK), 1), gx, gz)
    hit = want == target_col
    for q in range(4):
        chosen = jnp.where(hit & (quarter == q), 1.0, 0.0).astype(BF16)
        cols = pl.ds(q * QUART, QUART)
        grad[:, cols] = jnp.dot(chosen, ret[:, 0:QUART], preferred_element_type=F32).astype(BF16)
        start(grad.at[:, cols], grad_hbm.at[:, cols])
        if q == 0:
            pair = jnp.dot(chosen, ret[:, QUART:], preferred_element_type=F32)
            total = jnp.sum(jnp.where((iota(pair.shape, 1) & 63) == 0, pair, 0.0), axis=1, keepdims=True)
            total = jnp.sum(jnp.where(eye, total, 0.0), axis=0, keepdims=True)
            scaled = total / jnp.where(gate > 0.0, gate, 1.0)
            gate_grad[...] = jnp.where(ids[...] < NODES, scaled, 0.0)
    for copy in copies:
        copy.wait()


def body(tokens, out_grad, route_ids, route_gates, w_gate, w_up, w_down):
    any_space = pl.BlockSpec(memory_space=pl.ANY)
    in_vmem = pl.BlockSpec(memory_space=pltpu.VMEM)
    ids, gates = route_ids.T, route_gates.T
    copies = 30 + 8 * 7 + 6 + 4 + 4 * 6 + 15 + 1 + 10
    ret, ggu, gd = pl.pallas_call(
        exchange_kernel,
        out_shape=(
            pltpu.VMEM((TOK, QUART + SCW), BF16),
            pltpu.VMEM((2 * D, FFD), BF16),
            pltpu.VMEM((FFD, D), BF16),
        ),
        in_specs=[any_space] * 7,
        out_specs=(in_vmem,) * 3,
        scratch_shapes=[
            pltpu.VMEM((8, TOK), jnp.int32),
            pltpu.VMEM((8, TOK), BF16),
            pltpu.VMEM((TOK, D), BF16),
            pltpu.VMEM((TOK, D), BF16),
            pltpu.VMEM((8, TOK, TOK), BF16),
            pltpu.VMEM((2, TOK, QUART), BF16),
            pltpu.VMEM((2, TOK, QUART), BF16),
            pltpu.VMEM((2, 8, 64, QUART), BF16),
            pltpu.VMEM((2, PH * ROWS, D), BF16),
            pltpu.VMEM((D, 2 * FFD), BF16),
            pltpu.VMEM((D, 2 * FFD), BF16),
            pltpu.VMEM((FFD, D), BF16),
            pltpu.VMEM((PH, 64, 2 * FFD), BF16),
            pltpu.VMEM((2 * FFD, PH * ROWS), BF16),
            pltpu.VMEM((FFD, PH * ROWS), BF16),
            pltpu.VMEM((PH, 64, SCW), F32),
            pltpu.VMEM((PH, 64, 2 * FFD + SCW), BF16),
            pltpu.VMEM((PH, 64, 2 * FFD + SCW), BF16),
            pltpu.VMEM((3, 48, RW), F32),
            pltpu.VMEM((PH, 16, RW), BF16),
            pltpu.VMEM((PH, 16, RW), BF16),
            pltpu.VMEM((PH, 16, RW), BF16),
            pltpu.VMEM((PH, 16, RW), BF16),
            pltpu.VMEM((PH, 16, RW), BF16),
            pltpu.VMEM((PH, 16, RW), BF16),
            pltpu.VMEM((64, QUART + SCW), BF16),
            pltpu.VMEM((TOK, QUART + SCW), BF16),
            pltpu.VMEM((64, 64), BF16),
            pltpu.VMEM((ROWS, 2 * FFD), F32),
            pltpu.SemaphoreType.DMA((copies,)),
            pltpu.SemaphoreType.DMA((copies,)),
            pltpu.SemaphoreType.DMA((9,)),
        ],
        compiler_params=pltpu.CompilerParams(
            collective_id=0, has_side_effects=True, vmem_limit_bytes=52 * 2**20
        ),
        cost_estimate=pl.CostEstimate(
            flops=8 * 10**9, bytes_accessed=20 * 10**6, transcendentals=65536
        ),
        name="exchange",
    )(ids, gates, tokens, out_grad, w_gate[0], w_up[0], w_down[0])
    token_grad, gate_grad, gg, gu, gd = pl.pallas_call(
        scatter_kernel,
        out_shape=(
            jax.ShapeDtypeStruct((TOK, D), BF16),
            jax.ShapeDtypeStruct((8, TOK), F32),
            jax.ShapeDtypeStruct((D, FFD), BF16),
            jax.ShapeDtypeStruct((D, FFD), BF16),
            jax.ShapeDtypeStruct((FFD, D), BF16),
        ),
        in_specs=[in_vmem] * 5,
        out_specs=(any_space, in_vmem) + (any_space,) * 3,
        scratch_shapes=[
            pltpu.VMEM((TOK, D), BF16),
            pltpu.SemaphoreType.DMA((7,)),
        ],
        compiler_params=pltpu.CompilerParams(vmem_limit_bytes=16 * 2**20),
        name="scatter",
    )(ids, gates, *(pltpu.with_memory_space_constraint(x, pltpu.VMEM) for x in (ret, ggu, gd)))
    return token_grad, gate_grad.T, gg[None], gu[None], gd[None]


def solution(mesh):
    return jax.shard_map(
        body,
        mesh=mesh,
        in_specs=(
            P(("node", "local"), None),
            P(("node", "local"), None),
            P(("node", "local"), None),
            P(("node", "local"), None),
            P("node", None, "local"),
            P("node", None, "local"),
            P("node", "local", None),
        ),
        out_specs=(
            P(("node", "local"), None),
            P(("node", "local"), None),
            P("node", None, "local"),
            P("node", None, "local"),
            P("node", "local", None),
        ),
        check_vma=False,
    )
```

```python
import functools

import jax
import jax.numpy as jnp
from jax import lax
from jax.experimental import pallas as pl
from jax.experimental.pallas import tpu as pltpu
from jax.sharding import PartitionSpec as P

MESH = pl.DeviceIdType.MESH
F32 = jnp.float32
BF16 = jnp.bfloat16

CAP = 4
TOK = 256
D = 7168
HALF = D // 2
QUART = D // 4
FFD = 128
NODES = 16
SIDE = 4
SCW = 128
RW = D + SCW
PH = 4
OFFSETS = (
    (0, 0), (1, 1), (3, 3), (1, 3), (3, 1), (0, 2), (2, 0), (2, 2),
    (1, 2), (3, 2), (2, 1), (2, 3), (0, 1), (0, 3), (1, 0), (3, 0),
)


def two_bits(values):
    word = sum(v << (2 * i) for i, v in enumerate(values))
    return word - 2**32 if word >= 2**31 else word


DX_BITS = two_bits([dx for dx, _ in OFFSETS])
DZ_BITS = two_bits([dz for _, dz in OFFSETS])
ROWS = 128


def iota(shape, dim):
    return lax.broadcasted_iota(jnp.int32, shape, dim)


def slot_targets(ids, gates):
    held = ids < NODES
    expert = jnp.sum(jnp.where(held, ids, 0).astype(F32), axis=0, keepdims=True)
    inside = jnp.sum(jnp.where(held, 1.0, 0.0), axis=0, keepdims=True) > 0.5
    gate = jnp.sum(jnp.where(held, gates.astype(F32), 0.0), axis=0, keepdims=True)
    row = iota((NODES, TOK), 0).astype(F32)
    one_hot = jnp.where((row == expert) & inside, 1.0, 0.0)
    before = jnp.where(iota((TOK, TOK), 0) < iota((TOK, TOK), 1), 1.0, 0.0)
    ranks = jnp.dot(one_hot.astype(BF16), before.astype(BF16), preferred_element_type=F32)
    rank = jnp.sum(ranks * one_hot, axis=0, keepdims=True)
    target = jnp.where(inside, expert * CAP + rank, -1.0)
    return target, gate


def wanted(block, gx, gz):
    k = block >> 4
    dx = lax.shift_right_logical(jnp.full(k.shape, DX_BITS, jnp.int32), 2 * k) & 3
    dz = lax.shift_right_logical(jnp.full(k.shape, DZ_BITS, jnp.int32), 2 * k) & 3
    node = ((gx - dx) & 3) * SIDE + ((gz - dz) & 3)
    return (node * CAP + (block & 3)).astype(F32), (block >> 2) & 3


def hi_lo(score):
    hi = score.astype(BF16).astype(F32)
    lane = iota(score.shape, 1)
    return jnp.where(lane < 64, hi, score - hi).astype(BF16)


def from_hi_lo(pair):
    wide = pair.astype(F32)
    return wide + pltpu.roll(wide, 64, 1)


def contract_cols(left, right):
    return lax.dot_general(left, right, (((1,), (1,)), ((), ())), preferred_element_type=F32)


def exchange_kernel(
    ids_hbm, gates_hbm, tok_hbm, og_hbm, wg_hbm, wu_hbm, wd_hbm,
    retr, gguo, gdo,
    ids, gates, tok, og, pick, sraw, rraw, rx, xg, wgu, wgup, wd,
    dl, dlt, hidt, score, psend, precv,
    rgf, o3s, o3r, j1s, j1r, j2s, j2r, fstk, rets, perm, pre_ref,
    ssem, rsem, lsem,
):
    node = lax.axis_index("node")
    loc = lax.axis_index("local")
    gx, gz = node // SIDE, node % SIDE
    y, c = loc // 2, loc % 2
    up = (node, ((y + 1) % 4) * 2 + c)
    down = (node, ((y + 3) % 4) * 2 + c)
    other = (node, y * 2 + 1 - c)

    def dest(k):
        dx, dz = OFFSETS[k]
        return (((gx + 4 - dx) % 4) * SIDE + (gz + 4 - dz) % 4, loc)

    def source(k):
        dx, dz = OFFSETS[k]
        return (((gx + dx) % 4) * SIDE + (gz + dz) % 4, loc)

    barrier = pltpu.get_barrier_semaphore()
    partners = [up, down, other] + [dest(k) for k in range(1, NODES)]
    for who in partners:
        pl.semaphore_signal(barrier, inc=1, device_id=who, device_id_type=MESH)

    local = []

    def load(src, dst):
        copy = pltpu.make_async_copy(src, dst, lsem.at[len(local)])
        local.append(copy)
        copy.start()
        return copy

    ld_ids = load(ids_hbm, ids)
    ld_gates = load(gates_hbm, gates)
    ld_tok = load(tok_hbm, tok)

    remote = []

    def send(src, dst, who):
        i = len(remote)
        copy = pltpu.make_async_remote_copy(
            src_ref=src, dst_ref=dst, send_sem=ssem.at[i], recv_sem=rsem.at[i],
            device_id=who, device_id_type=MESH,
        )
        remote.append(copy)
        copy.start()
        return copy

    ld_ids.wait()
    ld_gates.wait()
    target, gate = slot_targets(ids[...], gates[...])
    want, quarter = wanted(iota((TOK, TOK), 0), gx, gz)
    hit = want == target
    for q in range(4):
        chosen = hit & (quarter == q)
        pick[q] = jnp.where(chosen, 1.0, 0.0).astype(BF16)
        pick[4 + q] = jnp.where(chosen, gate, 0.0).astype(BF16)
    pi, pj = iota((64, 64), 0), iota((64, 64), 1)
    swapped = ((pj >> 2) & 3) * 16 + (pj >> 4) * 4 + (pj & 3)
    perm[...] = jnp.where(pi == swapped, 1.0, 0.0).astype(BF16)

    def pick_rows(a, rows, lo, hi):
        @pl.loop(0, QUART // 256)
        def _(t):
            acc = jnp.zeros((hi - lo, 256), F32)
            for q in range(4):
                cols = pl.ds(pl.multiple_of(q * QUART + t * 256, 256), 256)
                acc += jnp.dot(pick[4 * a + q, lo:hi, :], rows[:, cols], preferred_element_type=F32)
            cols = pl.ds(pl.multiple_of(t * 256, 256), 256)
            sraw[a, lo:hi, cols] = acc.astype(BF16)
            if lo == 0:
                rx[a, 0, 0:16, cols] = acc[0:16].astype(BF16)

    scatter = {}

    def send_part(u):
        a, p = u % 2, u // 2
        for k in range(4 * p, 4 * p + 4):
            if k:
                part = pl.ds(16 * k, 16)
                land = rraw.at[a, part] if p else rx.at[a, 0, part]
                scatter[a, k] = send(sraw.at[a, part], land, dest(k))

    gath = {}

    def own_block(a, name, rows):
        block = rx.at[a, 0, rows]
        gath[a, "u" + name] = send(block, rx.at[a, 1, rows], up)
        gath[a, "d" + name] = send(block, rx.at[a, 2, rows], down)
        gath[a, "c0" + name] = send(block, rx.at[a, 4, rows], other)

    def rest(a):
        for k in range(1, 4):
            scatter[a, k].wait_recv()
        own_block(a, "", pl.ds(16, 48))

    ld_tok.wait()
    ld_og = load(og_hbm, og)
    pick_rows(0, tok, 0, 64)
    pl.semaphore_wait(barrier, len(partners))
    own_block(0, "first", pl.ds(0, 16))
    send_part(0)
    ld_og.wait()
    ld_wg = load(wg_hbm, wgu.at[:, pl.ds(0, FFD)])
    ld_wu = load(wu_hbm, wgu.at[:, pl.ds(FFD, FFD)])
    ld_wd = load(wd_hbm, wd)
    pick_rows(1, og, 0, 64)
    own_block(1, "first", pl.ds(0, 16))
    send_part(1)
    pick_rows(0, tok, 64, TOK)

    left, right = pl.ds(0, HALF), pl.ds(HALF, HALF)

    def unit(u):
        return u % 2, (u // 2) * ROWS

    def spread(u):
        a, at = unit(u)
        p = u // 2
        for k in range(4 * p, 4 * p + 4):
            if k:
                scatter[a, k].wait_recv()
        rows = jnp.dot(perm[...], rraw[a, 64 * p:64 * p + 64, :], preferred_element_type=F32).astype(BF16)
        for q in range(4):
            xg[a, at:at + 16, q * QUART:(q + 1) * QUART] = rows[16 * q:16 * q + 16]
        mine = xg.at[a, pl.ds(at, 16)]
        gath[u, "u"] = send(mine, xg.at[a, pl.ds(at + 16, 16)], up)
        gath[u, "d"] = send(mine, xg.at[a, pl.ds(at + 32, 16)], down)
        gath[u, "c0"] = send(mine, xg.at[a, pl.ds(at + 64, 16)], other)

    def forward(u):
        a, at = unit(u)
        if u < 2:
            near, far = pl.ds(0, QUART // 2), pl.ds(QUART // 2, QUART // 2)
            gath[u, "ufirst"].wait_recv()
            gath[u, "u"].wait_recv()
            gath[u, "fu"] = send(rx.at[a, 1, :, near], rx.at[a, 3, :, near], up)
            gath[u, "dfirst"].wait_recv()
            gath[u, "d"].wait_recv()
            gath[u, "fd"] = send(rx.at[a, 2, :, far], rx.at[a, 3, :, far], down)
            gath[u, "c12"] = send(rx.at[a, pl.ds(1, 2)], rx.at[a, pl.ds(5, 2)], other)
            return
        opp = pl.ds(at + 48, 16)
        gath[u, "u"].wait_recv()
        gath[u, "fu"] = send(xg.at[a, pl.ds(at + 16, 16), left], xg.at[a, opp, left], up)
        gath[u, "d"].wait_recv()
        gath[u, "fd"] = send(xg.at[a, pl.ds(at + 32, 16), right], xg.at[a, opp, right], down)
        gath[u, "c12"] = send(xg.at[a, pl.ds(at + 16, 32)], xg.at[a, pl.ds(at + 80, 32)], other)

    def opposite(u):
        a, at = unit(u)
        gath[u, "fu"].wait_recv()
        gath[u, "fd"].wait_recv()
        if u < 2:
            gath[u, "c3"] = send(rx.at[a, 3], rx.at[a, 7], other)
            return
        gath[u, "c3"] = send(xg.at[a, pl.ds(at + 48, 16)], xg.at[a, pl.ds(at + 112, 16)], other)

    back = {}

    def arrived(u):
        a, at = unit(u)
        for part in ("c0", "c12", "c3"):
            gath[u, part].wait_recv()
        if u < 2:
            gath[u, "c0first"].wait_recv()

            @pl.loop(0, 8)
            def _(b):
                rows = jnp.dot(perm[...], rx[a, b], preferred_element_type=F32).astype(BF16)
                to = pl.ds(pl.multiple_of(b * 16, 16), 16)
                for q in range(4):
                    xg[a, to, q * QUART:(q + 1) * QUART] = rows[16 * q:16 * q + 16]

    def project(p):
        arrived(2 * p)
        at = p * ROWS
        pre_ref[...] = jnp.dot(xg[0, at:at + ROWS, :], wgu[...], preferred_element_type=F32)

    def compute(p):
        arrived(2 * p + 1)
        at = p * ROWS
        pre = pre_ref[...]
        hidden_grad = contract_cols(xg[1, at:at + ROWS, :], wd[...])
        gate_pre, up_pre = pre[:, :FFD], pre[:, FFD:]
        logistic = jax.nn.sigmoid(gate_pre)
        silu = gate_pre * logistic
        hidden = (silu * up_pre).astype(BF16).astype(F32)
        gate_delta = hidden_grad * up_pre * logistic * (1.0 + gate_pre * (1.0 - logistic))
        up_delta = hidden_grad * silu
        part = jnp.sum(hidden * hidden_grad, axis=1, keepdims=True)
        part = jnp.broadcast_to(part, (ROWS, SCW))
        psend[p, :, 0:FFD] = gate_delta[64:128].astype(BF16)
        psend[p, :, FFD:2 * FFD] = up_delta[64:128].astype(BF16)
        psend[p, :, 2 * FFD:] = hi_lo(part[64:128])
        back[p, "c"] = send(psend.at[p], precv.at[p], other)
        score[p] = part[0:64]
        dl[p, :, 0:FFD] = gate_delta[0:64].astype(BF16)
        dl[p, :, FFD:2 * FFD] = up_delta[0:64].astype(BF16)
        dlt[0:FFD, at:at + ROWS] = gate_delta.T.astype(BF16)
        dlt[FFD:2 * FFD, at:at + ROWS] = up_delta.T.astype(BF16)
        hidt[:, at:at + ROWS] = hidden.T.astype(BF16)

    tail = pl.ds(HALF, RW - HALF)

    def row_tiles(p, lo, hi, ready):
        mine, theirs = dl[p], precv[p, :, 0:2 * FFD]

        @pl.loop(lo, hi)
        def _(t):
            cols = pl.ds(pl.multiple_of(t * 512, 512), 512)
            grad = contract_cols(mine, wgu[cols, :]) + contract_cols(theirs, wgup[cols, :])
            rgf[p % 3, :, cols] = grad[0:48]
            o3s[p, :, cols] = grad[48:64].astype(BF16)
            ready[p, :, cols] = grad[16:32].astype(BF16) if ready is j1s else grad[32:48].astype(BF16)

    def row_left(p):
        back[p, "c"].wait_recv()
        total = score[p] + from_hi_lo(precv[p, :, 2 * FFD:])
        rgf[p % 3, :, D:] = total[0:48]
        o3s[p, :, D:] = hi_lo(total[48:64])
        j2s[p, :, D:] = hi_lo(total[32:48])
        row_tiles(p, 0, 7, j1s)

    def row_right(p):
        row_tiles(p, 7, 14, j2s)

    def send_left(p):
        back[p, "ol"] = send(o3s.at[p, :, left], o3r.at[p, :, left], up)
        back[p, "j1l"] = send(j1s.at[p, :, left], j1r.at[p, :, left], down)

    def send_right(p):
        back[p, "or"] = send(o3s.at[p, :, tail], o3r.at[p, :, tail], down)
        back[p, "j2r"] = send(j2s.at[p, :, tail], j2r.at[p, :, tail], up)

    def row_grads(p):
        row_left(p)
        send_left(p)
        row_right(p)
        send_right(p)

    def merge(p):
        back[p, "ol"].wait_recv()
        j2s[p, :, 0:HALF] = (rgf[p % 3, 32:48, 0:HALF] + o3r[p, :, 0:HALF].astype(F32)).astype(BF16)
        back[p, "j2l"] = send(j2s.at[p, :, left], j2r.at[p, :, left], up)
        back[p, "or"].wait_recv()
        j1s[p, :, HALF:D] = (rgf[p % 3, 16:32, HALF:D] + o3r[p, :, HALF:D].astype(F32)).astype(BF16)
        j1s[p, :, D:] = hi_lo(rgf[p % 3, 16:32, D:] + from_hi_lo(o3r[p, :, D:]))
        back[p, "j1r"] = send(j1s.at[p, :, tail], j1r.at[p, :, tail], down)

    def home(p):
        for part in ("j1l", "j1r", "j2l", "j2r"):
            back[p, part].wait_recv()
        for q in range(4):
            cols = slice(q * QUART, (q + 1) * QUART)
            full = rgf[p % 3, 0:16, cols] + j1r[p, :, cols].astype(F32) + j2r[p, :, cols].astype(F32)
            fstk[16 * q:16 * q + 16, 0:QUART] = full.astype(BF16)
        total = hi_lo(rgf[p % 3, 0:16, D:] + from_hi_lo(j1r[p, :, D:]) + from_hi_lo(j2r[p, :, D:]))
        for q in range(4):
            fstk[16 * q:16 * q + 16, QUART:] = total
        block = jnp.dot(perm[...], fstk[...], preferred_element_type=F32).astype(BF16)
        rets[64 * p:64 * p + 64, :] = block
        if p == 0:
            retr[0:16, :] = block[0:16]
        for k in range(4 * p, 4 * p + 4):
            if k:
                part = pl.ds(16 * k, 16)
                back[k] = send(rets.at[part], retr.at[part], source(k))

    def half_quarter(q, piece, score):
        at = q * QUART + piece * (QUART // 2)
        return slice(at, at + QUART // 2 + (SCW if score else 0))

    def merge_pieces(p):
        for piece in range(2):
            if piece == 0:
                back[p, "ol"].wait_recv()
            for q in range(2):
                cols = half_quarter(q, piece, False)
                j2s[p, :, cols] = (rgf[p % 3, 32:48, cols] + o3r[p, :, cols].astype(F32)).astype(BF16)
                back[p, "j2l", piece, q] = send(j2s.at[p, :, cols], j2r.at[p, :, cols], up)
            if piece == 0:
                back[p, "or"].wait_recv()
            for q in range(2, 4):
                cols = half_quarter(q, piece, False)
                j1s[p, :, cols] = (rgf[p % 3, 16:32, cols] + o3r[p, :, cols].astype(F32)).astype(BF16)
                score_too = piece == 1 and q == 3
                if score_too:
                    j1s[p, :, D:] = hi_lo(rgf[p % 3, 16:32, D:] + from_hi_lo(o3r[p, :, D:]))
                cols = half_quarter(q, piece, score_too)
                back[p, "j1r", piece, q] = send(j1s.at[p, :, cols], j1r.at[p, :, cols], down)

    def home_piece(p, piece):
        if piece == 0:
            back[p, "j1l"].wait_recv()
            back[p, "j2r"].wait_recv()
        for q in range(4):
            back[(p, "j2l", piece, q) if q < 2 else (p, "j1r", piece, q)].wait_recv()
            cols = half_quarter(q, piece, False)
            full = rgf[p % 3, 0:16, cols] + j1r[p, :, cols].astype(F32) + j2r[p, :, cols].astype(F32)
            fstk[16 * q:16 * q + 16, half_quarter(0, piece, False)] = full.astype(BF16)
        if piece == 1:
            total = hi_lo(rgf[p % 3, 0:16, D:] + from_hi_lo(j1r[p, :, D:]) + from_hi_lo(j2r[p, :, D:]))
            for q in range(4):
                fstk[16 * q:16 * q + 16, QUART:] = total
        cols = half_quarter(0, piece, piece == 1)
        block = jnp.dot(perm[...], fstk[:, cols], preferred_element_type=F32).astype(BF16)
        rets[64 * p:64 * p + 64, cols] = block
        for k in range(4 * p, 4 * p + 4):
            part = pl.ds(16 * k, 16)
            back[k, piece] = send(rets.at[part, cols], retr.at[part, cols], source(k))

    def weight_grads(lo, hi):
        @pl.loop(lo, hi)
        def _(t):
            cols = pl.ds(pl.multiple_of(t * 512, 512), 512)
            both = jnp.dot(dlt[...], xg[0, :, cols], preferred_element_type=F32)
            gguo[cols, :] = both[0:FFD].T.astype(BF16)
            gguo[pl.ds(pl.multiple_of(D + t * 512, 512), 512), :] = both[FFD:].T.astype(BF16)
            gdo[:, cols] = jnp.dot(hidt[...], xg[1, :, cols], preferred_element_type=F32).astype(BF16)

    send_part(2)
    rest(0)
    pick_rows(1, og, 64, TOK)
    send_part(3)
    rest(1)
    ld_wg.wait()
    ld_wu.wait()
    ld_wd.wait()
    forward(0)
    spread(2)
    send_part(4)
    forward(1)
    opposite(0)
    spread(3)
    send_part(5)
    weights = send(wgu, wgup, other)
    forward(2)
    opposite(1)
    project(0)
    compute(0)
    spread(4)
    send_part(6)
    forward(3)
    opposite(2)
    spread(5)
    send_part(7)
    weights.wait_recv()
    row_grads(0)
    forward(4)
    opposite(3)
    project(1)
    compute(1)
    spread(6)
    merge(0)
    forward(5)
    opposite(4)
    spread(7)
    row_grads(1)
    home(0)
    forward(6)
    opposite(5)
    project(2)
    compute(2)
    forward(7)
    opposite(6)
    row_left(2)
    row_right(2)
    project(3)
    merge(1)
    opposite(7)
    send_left(2)
    send_right(2)
    compute(3)
    merge(2)
    row_left(3)
    send_left(3)
    row_right(3)
    send_right(3)
    home(1)
    home(2)
    merge_pieces(3)
    weight_grads(0, 10)
    home_piece(3, 0)
    home_piece(3, 1)
    weight_grads(10, 14)
    for k in range(1, 12):
        back[k].wait_recv()
    for k in range(12, NODES):
        back[k, 0].wait_recv()
        back[k, 1].wait_recv()
    for copy in remote:
        copy.wait_send()


def scatter_kernel(ids, gates, ret, ggu, gd_in, grad_hbm, gate_grad, gg, gu, gd, grad, sem):
    copies = []

    def start(src, dst):
        copy = pltpu.make_async_copy(src, dst, sem.at[len(copies)])
        copies.append(copy)
        copy.start()

    start(ggu.at[pl.ds(0, D)], gg)
    start(ggu.at[pl.ds(D, D)], gu)
    start(gd_in, gd)
    node = lax.axis_index("node")
    gx, gz = node // SIDE, node % SIDE
    target, gate = slot_targets(ids[...], gates[...])
    eye = iota((TOK, TOK), 0) == iota((TOK, TOK), 1)
    target_col = jnp.sum(jnp.where(eye, target, 0.0), axis=1, keepdims=True)
    want, quarter = wanted(iota((TOK, TOK), 1), gx, gz)
    hit = want == target_col
    for q in range(4):
        chosen = jnp.where(hit & (quarter == q), 1.0, 0.0).astype(BF16)
        cols = pl.ds(q * QUART, QUART)
        grad[:, cols] = jnp.dot(chosen, ret[:, 0:QUART], preferred_element_type=F32).astype(BF16)
        start(grad.at[:, cols], grad_hbm.at[:, cols])
        if q == 0:
            pair = jnp.dot(chosen, ret[:, QUART:], preferred_element_type=F32)
            total = jnp.sum(jnp.where((iota(pair.shape, 1) & 63) == 0, pair, 0.0), axis=1, keepdims=True)
            total = jnp.sum(jnp.where(eye, total, 0.0), axis=0, keepdims=True)
            scaled = total / jnp.where(gate > 0.0, gate, 1.0)
            gate_grad[...] = jnp.where(ids[...] < NODES, scaled, 0.0)
    for copy in copies:
        copy.wait()


def body(tokens, out_grad, route_ids, route_gates, w_gate, w_up, w_down):
    any_space = pl.BlockSpec(memory_space=pl.ANY)
    in_vmem = pl.BlockSpec(memory_space=pltpu.VMEM)
    ids, gates = route_ids.T, route_gates.T
    copies = 30 + 8 * 7 + 6 + 4 + 4 * 6 + 15 + 1 + 10
    ret, ggu, gd = pl.pallas_call(
        exchange_kernel,
        out_shape=(
            pltpu.VMEM((TOK, QUART + SCW), BF16),
            pltpu.VMEM((2 * D, FFD), BF16),
            pltpu.VMEM((FFD, D), BF16),
        ),
        in_specs=[any_space] * 7,
        out_specs=(in_vmem,) * 3,
        scratch_shapes=[
            pltpu.VMEM((8, TOK), jnp.int32),
            pltpu.VMEM((8, TOK), BF16),
            pltpu.VMEM((TOK, D), BF16),
            pltpu.VMEM((TOK, D), BF16),
            pltpu.VMEM((8, TOK, TOK), BF16),
            pltpu.VMEM((2, TOK, QUART), BF16),
            pltpu.VMEM((2, TOK, QUART), BF16),
            pltpu.VMEM((2, 8, 64, QUART), BF16),
            pltpu.VMEM((2, PH * ROWS, D), BF16),
            pltpu.VMEM((D, 2 * FFD), BF16),
            pltpu.VMEM((D, 2 * FFD), BF16),
            pltpu.VMEM((FFD, D), BF16),
            pltpu.VMEM((PH, 64, 2 * FFD), BF16),
            pltpu.VMEM((2 * FFD, PH * ROWS), BF16),
            pltpu.VMEM((FFD, PH * ROWS), BF16),
            pltpu.VMEM((PH, 64, SCW), F32),
            pltpu.VMEM((PH, 64, 2 * FFD + SCW), BF16),
            pltpu.VMEM((PH, 64, 2 * FFD + SCW), BF16),
            pltpu.VMEM((3, 48, RW), F32),
            pltpu.VMEM((PH, 16, RW), BF16),
            pltpu.VMEM((PH, 16, RW), BF16),
            pltpu.VMEM((PH, 16, RW), BF16),
            pltpu.VMEM((PH, 16, RW), BF16),
            pltpu.VMEM((PH, 16, RW), BF16),
            pltpu.VMEM((PH, 16, RW), BF16),
            pltpu.VMEM((64, QUART + SCW), BF16),
            pltpu.VMEM((TOK, QUART + SCW), BF16),
            pltpu.VMEM((64, 64), BF16),
            pltpu.VMEM((ROWS, 2 * FFD), F32),
            pltpu.SemaphoreType.DMA((copies,)),
            pltpu.SemaphoreType.DMA((copies,)),
            pltpu.SemaphoreType.DMA((9,)),
        ],
        compiler_params=pltpu.CompilerParams(
            collective_id=0, has_side_effects=True, vmem_limit_bytes=52 * 2**20
        ),
        cost_estimate=pl.CostEstimate(
            flops=8 * 10**9, bytes_accessed=20 * 10**6, transcendentals=65536
        ),
        name="exchange",
    )(ids, gates, tokens, out_grad, w_gate[0], w_up[0], w_down[0])
    token_grad, gate_grad, gg, gu, gd = pl.pallas_call(
        scatter_kernel,
        out_shape=(
            jax.ShapeDtypeStruct((TOK, D), BF16),
            jax.ShapeDtypeStruct((8, TOK), F32),
            jax.ShapeDtypeStruct((D, FFD), BF16),
            jax.ShapeDtypeStruct((D, FFD), BF16),
            jax.ShapeDtypeStruct((FFD, D), BF16),
        ),
        in_specs=[in_vmem] * 5,
        out_specs=(any_space, in_vmem) + (any_space,) * 3,
        scratch_shapes=[
            pltpu.VMEM((TOK, D), BF16),
            pltpu.SemaphoreType.DMA((7,)),
        ],
        compiler_params=pltpu.CompilerParams(vmem_limit_bytes=16 * 2**20),
        name="scatter",
    )(ids, gates, *(pltpu.with_memory_space_constraint(x, pltpu.VMEM) for x in (ret, ggu, gd)))
    return token_grad, gate_grad.T, gg[None], gu[None], gd[None]


def solution(mesh):
    return jax.shard_map(
        body,
        mesh=mesh,
        in_specs=(
            P(("node", "local"), None),
            P(("node", "local"), None),
            P(("node", "local"), None),
            P(("node", "local"), None),
            P("node", None, "local"),
            P("node", None, "local"),
            P("node", "local", None),
        ),
        out_specs=(
            P(("node", "local"), None),
            P(("node", "local"), None),
            P("node", None, "local"),
            P("node", None, "local"),
            P("node", "local", None),
        ),
        check_vma=False,
    )
```
